32 devices in a mesh: dp: 16 (over z, y, core), head: 2 (over x).
Axes of the slice: x: 2, y: 2, z: 4, core: 2. Of those that a mesh axis runs over, the one named last changes fastest.
Arguments:
- tokens: bfloat16 [32768, 768], P(('dp', 'head')), may hold values from -6 to 6
- lengths: int32 [16, 4], P('dp'), may hold values from 0 to 2048, as said below
- feature_map: bfloat16 [12, 64, 256], replicated, may hold values from -5 to 5
- qkv_weight: bfloat16 [768, 3, 768], replicated, may hold values from -0.21875 to 0.21875
- qkv_bias: float32 [3, 768], replicated, may hold values from -3 to 3
- out_weight: bfloat16 [768, 768], replicated, may hold values from -0.875 to 0.875
- out_bias: float32 [768], replicated, may hold values from -2 to 2
- ln1_gain: float32 [768], replicated, may hold values from 0.5 to 1.5
- ln1_shift: float32 [768], replicated, may hold values from -2 to 2
- up_weight: bfloat16 [768, 3072], replicated, may hold values from -0.21875 to 0.21875
- up_bias: float32 [3072], replicated, may hold values from -3 to 3
- down_weight: bfloat16 [768, 3072], replicated, may hold values from -0.109375 to 0.109375
- down_bias: float32 [768], replicated, may hold values from -2 to 2
- ln2_gain: float32 [768], replicated, may hold values from 0.5 to 1.5
- ln2_shift: float32 [768], replicated, may hold values from -2 to 2
- cotangent: bfloat16 [32768, 768], P(('dp', 'head')), may hold values from -6 to 6
Outputs:
- output: bfloat16 [32768, 768], P(('dp', 'head'))
- grad_tokens: bfloat16 [32768, 768], P(('dp', 'head'))
- grad_qkv_weight: float32 [768, 3, 768], P('dp', None, 'head')
- grad_qkv_bias: float32 [3, 768], replicated
- grad_out_weight: float32 [768, 768], P('dp', 'head')
- grad_out_bias: float32 [768], replicated
- grad_ln1_gain: float32 [768], replicated
- grad_ln1_shift: float32 [768], replicated
- grad_up_weight: float32 [768, 3072], P('dp', 'head')
- grad_up_bias: float32 [3072], replicated
- grad_down_weight: float32 [768, 3072], P('dp', 'head')
- grad_down_bias: float32 [768], replicated
- grad_ln2_gain: float32 [768], replicated
- grad_ln2_shift: float32 [768], replicated
The draws below stay inside these ranges and needn't reach their ends.
Inputs may be any that keep to these rules, and one draw needn't show every extreme that they name: Each packed row of 2048 slots holds up to 4 sequences in order (a length may be 0), then padding; a row's lengths sum to at most 2048; in every row one sequence is longer than 1024 and covers slots 2048 // 2 - 1 and 1024, its place among the 4 varying from row to row; in some row one sequence fills all 2048 slots.
All inputs are finite; a program needn't handle non-finite values.
Results may differ from the reference program's by a relative error of at most 0.025.
Values may be sent and summed in bfloat16 or wider, within the bound.
No kernel may reach another device: no remote copies, remote signals or barrier semaphores. Data moves between devices by JAX's collectives and lax.ppermute only.
A program may use at most 256 MiB of HBM per device.

```python
import jax
import jax.numpy as jnp
from jax import lax

D = 768
HEADS = 12
HDIM = 64
FF = 3072
FEAT = 256
NSEG = 4
ROW = 2048
ROWS = 16
TOKENS = 32768


def draw_lengths(key, part):
    key = jax.random.fold_in(key, 7)
    short_key, pad_key, place_key, whole_key = jax.random.split(key, 4)
    shorts = jax.random.randint(short_key, (ROWS, NSEG), 0, ROW // 16)
    padding = jax.random.randint(pad_key, (ROWS, 1), 0, ROW // 8)
    longest_at = jax.random.randint(place_key, (ROWS, 1), 0, NSEG)
    single_row = jax.random.randint(whole_key, (), 0, ROWS)
    columns = jnp.arange(NSEG, dtype=jnp.int32)[None, :]
    row_index = jnp.arange(ROWS, dtype=jnp.int32)[:, None]
    packed = (row_index != single_row).astype(jnp.int32)
    shorts = shorts * packed * (columns != longest_at).astype(jnp.int32)
    padding = padding * packed
    longest = ROW - padding - jnp.sum(shorts, axis=1, keepdims=True)
    return jnp.where(columns == longest_at, longest, shorts).astype(jnp.int32)


def spiked(entries, rng, source, target, shards_of, factor):
    def block_of(dim):
        return (jnp.arange(entries.shape[dim]) // (entries.shape[dim] // shards_of)).reshape((-1,) + (1,) * (entries.ndim - 1 - dim))

    near = jax.random.permutation(rng, shards_of)[block_of(target)]
    far = (block_of(target) + shards_of // 2) % shards_of
    return jnp.where((block_of(source) == near) | (block_of(source) == far), factor * entries, entries)


def shard_levels(key, dims, shards, smallest, high):
    loudness = 1.0
    for axis_at, blocks in shards:
        draws = jax.random.uniform(jax.random.fold_in(jax.random.fold_in(key, 6), axis_at), (blocks,), jnp.float32, smallest / len(shards), high / len(shards))
        loudness = loudness * jnp.repeat(jnp.exp(draws), dims[axis_at] // blocks).reshape((-1,) + (1,) * (len(dims) - 1 - axis_at))
    return loudness


def noise(own_key, shape, scale, bound, shards=(), held_as=jnp.bfloat16):
    gain = shard_levels(own_key, shape, shards, -0.22, 0.18) if shards else 1.0
    entries = jax.random.normal(own_key, shape, jnp.float32) * scale * gain
    return jnp.minimum(jnp.maximum(entries, -bound), bound).astype(held_as)


def gaussian_with(rng, extent, scale, bound, shards, heavy, held_as=jnp.bfloat16):
    entries = scale * jax.random.normal(rng, extent, jnp.float32)
    if shards:
        entries = entries * shard_levels(rng, extent, shards, -0.22, 0.18)
    return jnp.clip(spiked(entries, jax.random.fold_in(rng, 3), *heavy), -bound, bound).astype(held_as)


def setup_inputs(seed: int = 0) -> dict:
    key_of = jax.random.split(jax.random.key(seed), 17)
    tokens = gaussian_with(key_of[0], (TOKENS, D), 1.0, 6.0, ((0, 32),), (0, 1, 32, 2.75))
    lengths = draw_lengths(jax.random.fold_in(key_of[16], 71), 0)
    feature_map = noise(key_of[2], (HEADS, HDIM, FEAT), 1.0, 5.0)
    qkv_weight = noise(key_of[3], (D, 3, D), D ** -0.5, 0.21875)
    qkv_bias = noise(key_of[4], (3, D), 0.5, 3.0, (), jnp.float32)
    out_weight = noise(key_of[5], (D, D), (D // 16) ** -0.5, 0.875)
    out_bias = noise(key_of[6], (D,), 0.3, 2.0, (), jnp.float32)
    ln1_gain = jnp.clip(1.0 + 0.1 * jax.random.normal(key_of[7], (D,), jnp.float32), 0.5, 1.5)
    ln1_shift = noise(key_of[8], (D,), 0.3, 2.0, (), jnp.float32)
    up_weight = noise(key_of[9], (D, FF), D ** -0.5, 0.21875)
    up_bias = noise(key_of[10], (FF,), 0.5, 3.0, (), jnp.float32)
    down_weight = noise(key_of[11], (D, FF), FF ** -0.5, 0.109375)
    down_bias = noise(key_of[12], (D,), 0.3, 2.0, (), jnp.float32)
    ln2_gain = jnp.clip(1.0 + 0.1 * jax.random.normal(key_of[13], (D,), jnp.float32), 0.5, 1.5)
    ln2_shift = noise(key_of[14], (D,), 0.3, 2.0, (), jnp.float32)
    cotangent = gaussian_with(key_of[15], (TOKENS, D), 1.0, 6.0, ((0, 32),), (0, 1, 32, 2.75))
    return {"tokens": tokens, "lengths": lengths, "feature_map": feature_map, "qkv_weight": qkv_weight, "qkv_bias": qkv_bias, "out_weight": out_weight, "out_bias": out_bias, "ln1_gain": ln1_gain, "ln1_shift": ln1_shift, "up_weight": up_weight, "up_bias": up_bias, "down_weight": down_weight, "down_bias": down_bias, "ln2_gain": ln2_gain, "ln2_shift": ln2_shift, "cotangent": cotangent}


@jax.custom_vjp
def low(v):
    return lax.optimization_barrier(v.astype(jnp.bfloat16)).astype(jnp.float32)

@jax.custom_vjp
def low_back(v):
    return v

def low_keep(v):
    return (low(v), None)

def low_pass(kept, grad):
    return (grad,)

def back_keep(v):
    return (v, None)

def back_low(kept, grad):
    return (low(grad),)
low.defvjp(low_keep, low_pass)
low_back.defvjp(back_keep, back_low)
highest = lax.Precision.HIGHEST
norm_epsilon = 1e-06

def layer_norm(values, norm_gain, norm_shift):
    centred = values - lax.optimization_barrier(jnp.mean(values, axis=-1, keepdims=True))
    spread = lax.optimization_barrier(jnp.mean(centred * centred, axis=-1, keepdims=True))
    return centred * lax.rsqrt(spread + norm_epsilon) * norm_gain + norm_shift

def member_table(row_lengths):
    seq_ends = jnp.cumsum(row_lengths).astype(jnp.int32)
    seq_starts = seq_ends - row_lengths.astype(jnp.int32)
    positions = jnp.arange(ROW, dtype=jnp.int32)[:, None]
    inside = jnp.logical_and(positions >= seq_starts[None, :], positions < seq_ends[None, :])
    return inside.astype(jnp.float32)

def row_forward(row_tokens, members, is_live, feature_map, qkv_weight, qkv_bias, out_weight, out_bias, ln1_gain, ln1_shift, up_weight, up_bias, down_weight, down_bias, ln2_gain, ln2_shift):
    factor = HDIM ** (-0.25)
    projected = jnp.einsum('te,ecf->ctf', row_tokens, qkv_weight, precision=highest) + qkv_bias[:, None, :]
    rounded = low(low_back(projected)).reshape(3, ROW, HEADS, HDIM)
    queries, key_rows, value_rows = (rounded[0], rounded[1], rounded[2])
    query_logits = low_back(factor * jnp.einsum('thd,hdm->thm', queries, feature_map, precision=highest) - 0.5 * factor * factor * lax.optimization_barrier(jnp.sum(queries * queries, axis=-1, keepdims=True)))
    key_logits = low_back(factor * jnp.einsum('thd,hdm->thm', key_rows, feature_map, precision=highest) - 0.5 * factor * factor * lax.optimization_barrier(jnp.sum(key_rows * key_rows, axis=-1, keepdims=True)))
    query_features = low(jnp.exp(query_logits - lax.optimization_barrier(jnp.max(query_logits, axis=-1, keepdims=True))))
    key_features = low(jnp.exp(key_logits))
    segment_state = low(low_back(jnp.einsum('ts,thm,thd->shmd', members, key_features, value_rows, precision=highest)))
    segment_total = low(low_back(jnp.einsum('ts,thm->shm', members, key_features, precision=highest)))
    numerator = low_back(jnp.einsum('ts,thm,shmd->thd', members, query_features, segment_state, precision=highest))
    denominator = low_back(jnp.einsum('ts,thm,shm->th', members, query_features, segment_total, precision=highest) + (1.0 - is_live)[:, None])
    mixed_rows = low((numerator / denominator[:, :, None]).reshape(ROW, D))
    attended = low_back(jnp.dot(mixed_rows, out_weight.T, precision=highest))
    hidden = row_tokens + attended + out_bias
    normed = layer_norm(hidden, ln1_gain, ln1_shift)
    up_pre = low_back(jnp.dot(low(normed), up_weight, precision=highest) + up_bias)
    activated = low(jax.nn.gelu(up_pre, approximate=False))
    branch = low_back(jnp.dot(activated, down_weight.T, precision=highest))
    return layer_norm(normed + branch + down_bias, ln2_gain, ln2_shift)

def reference(tokens, lengths, feature_map, qkv_weight, qkv_bias, out_weight, out_bias, ln1_gain, ln1_shift, up_weight, up_bias, down_weight, down_bias, ln2_gain, ln2_shift, cotangent):
    weights_f32 = tuple((weight.astype(jnp.float32) for weight in (qkv_weight, qkv_bias, out_weight, out_bias, ln1_gain, ln1_shift, up_weight, up_bias, down_weight, down_bias, ln2_gain, ln2_shift)))
    map_f32 = feature_map.astype(jnp.float32)
    row_tokens = tokens.astype(jnp.float32).reshape(ROWS, ROW, D)
    row_cot = cotangent.astype(jnp.float32).reshape(ROWS, ROW, D)

    def row_step(totals, inputs):
        one_row, one_cot, row_lengths = inputs
        members = member_table(row_lengths)
        is_live = lax.optimization_barrier(jnp.sum(members, axis=1))

        def forward(values, *weights):
            return row_forward(values, members, is_live, map_f32, *weights)
        row_output, pullback = jax.vjp(forward, one_row, *weights_f32)
        gradients = pullback(one_cot)
        totals = tuple((running + update for running, update in zip(totals, gradients[1:])))
        return (totals, (row_output.astype(jnp.bfloat16), gradients[0].astype(jnp.bfloat16)))
    zero_totals = tuple((jnp.zeros(weight.shape, jnp.float32) for weight in weights_f32))
    totals, (outputs, grad_rows) = lax.scan(row_step, zero_totals, (row_tokens, row_cot, lengths))
    return (outputs.reshape(TOKENS, D), grad_rows.reshape(TOKENS, D), totals[0], totals[1], totals[2], totals[3], totals[4], totals[5], totals[6], totals[7], totals[8], totals[9], totals[10], totals[11])
```

```python
import functools

import jax
import jax.numpy as jnp
from jax import lax
from jax.experimental import pallas as pl
from jax.experimental.pallas import tpu as pltpu
from jax.sharding import PartitionSpec as P

bf16 = jnp.bfloat16
f32 = jnp.float32
norm_epsilon = 1e-06
root_half = 0.7071067811865476
inv_root_tau = 0.3989422804014327
vmem_limit = 60 * 1024 * 1024
nt_dims = (((1,), (1,)), ((), ()))


def mm(a, b):
    return jnp.dot(a, b, preferred_element_type=f32)


def mm_nt(a, b):
    return lax.dot_general(a, b, nt_dims, preferred_element_type=f32)


def iota(shape, dim):
    return lax.broadcasted_iota(jnp.int32, shape, dim)


def bounds(len_ref, nseg):
    starts, ends, run = [], [], jnp.int32(0)
    for s in range(nseg):
        starts.append(run)
        run = run + len_ref[0, s]
        ends.append(run)
    return starts, ends


def spanning(ends, half):
    count = jnp.int32(0)
    for end in ends:
        count = count + (end < half).astype(jnp.int32)
    return count


def pick(index, values):
    out = jnp.full(index.shape, values[-1], jnp.int32)
    for s in range(len(values) - 2, -1, -1):
        out = jnp.where(index == s, values[s], out)
    return out


def inside(pos, index, starts, ends):
    return jnp.logical_and(pos >= pick(index, starts), pos < pick(index, ends))


def as_bf(mask):
    return jnp.where(mask, 1.0, 0.0).astype(bf16)


def split_hi_lo(v):
    hi = v.astype(bf16)
    lo = (v - hi.astype(f32)).astype(bf16)
    return jnp.concatenate([hi, lo], axis=1)


def masked_rows(rows_t, lane_masks, tail):
    return jnp.concatenate([rows_t * m for m in lane_masks] + [tail], axis=0)


def head_map(map_ref, h):
    m = map_ref[h]
    z = jnp.zeros_like(m)
    return jnp.concatenate([m, z] if h % 2 == 0 else [z, m], axis=0)


def key_offset(k_pair, low_half, j):
    sq = jnp.square(k_pair.astype(f32))
    mine = low_half if j == 0 else jnp.logical_not(low_half)
    return jnp.sum(jnp.where(mine, sq, 0.0), axis=-1, keepdims=True)


def put_states(own_ref, tot_ref, span_ref, recv_ref, st_ref, totp_ref, here, nseg, heads, hdim):
    wide = nseg * hdim
    feat = st_ref.shape[1]
    recv_tot = recv_ref[heads * hdim :, :].astype(f32)
    seg_row = iota((8, feat), 0)
    for h in range(heads):
        st_ref[h * wide : (h + 1) * wide, :] = own_ref[h * wide : (h + 1) * wide, :]
        both = span_ref[h * hdim : (h + 1) * hdim, :] + recv_ref[h * hdim : (h + 1) * hdim, :].astype(f32)
        at = pl.multiple_of(h * wide + here * hdim, hdim)
        st_ref[pl.ds(at, hdim), :] = both.astype(bf16)
        tot = tot_ref[8 * h : 8 * h + 8, :]
        tot = jnp.where(seg_row == here, tot + recv_tot[h : h + 1, :], tot)
        parts = [tot]
        if h > 0:
            parts.insert(0, jnp.zeros((8 * h, feat), f32))
        if 8 * h + 8 < 128:
            parts.append(jnp.zeros((128 - 8 * h - 8, feat), f32))
        totp_ref[128 * h : 128 * (h + 1), :] = jnp.concatenate(parts, axis=0).astype(bf16)


def emit_states(acc_ref, own_ref, tot_ref, span_ref, send_ref, here, nseg, heads, hdim):
    wide = nseg * hdim
    feat = acc_ref.shape[2]
    for h in range(heads):
        own_ref[h * wide : (h + 1) * wide, :] = acc_ref[h, 0:wide, :].astype(bf16)
        tot_ref[8 * h : 8 * h + 8, :] = acc_ref[h, wide : wide + 8, :]
        at = pl.multiple_of(here * hdim, hdim)
        part = acc_ref[h, pl.ds(at, hdim), :]
        span_ref[h * hdim : (h + 1) * hdim, :] = part
        send_ref[h * hdim : (h + 1) * hdim, :] = part.astype(bf16)
    row = iota((16, feat), 0)
    seg_row = iota((8, feat), 0)
    tots = jnp.zeros((16, feat), f32)
    for h in range(heads):
        mine = jnp.sum(jnp.where(seg_row == here, acc_ref[h, wide : wide + 8, :], 0.0), axis=0, keepdims=True)
        tots = jnp.where(row == h, mine, tots)
    send_ref[heads * hdim :, :] = tots.astype(bf16)


def lane_segment_masks(first, rows, hdim, starts, ends):
    pos = first + iota((hdim, rows), 1)
    masks = [as_bf(jnp.logical_and(pos >= a, pos < b)) for a, b in zip(starts, ends)]
    pos = first + iota((16, rows), 1)
    seg = iota((16, rows), 0)
    tail = as_bf(jnp.logical_and(seg < len(starts), inside(pos, seg, starts, ends)))
    return masks, tail


def forward_keys(
    len_ref, tok_ref, w_ref, b_ref, map_ref, qkv_ref, own_ref, tot_ref, span_ref, send_ref, acc_ref,
    *, half, nseg, heads, hdim, width
):
    step = pl.program_id(0)
    rows = tok_ref.shape[0]
    starts, ends = bounds(len_ref, nseg)
    here = spanning(ends, half)
    first = lax.axis_index("head") * half + step * rows
    factor = hdim ** (-0.25)

    @pl.when(step == 0)
    def _():
        acc_ref[...] = jnp.zeros_like(acc_ref)

    masks, tail = lane_segment_masks(first, rows, hdim, starts, ends)
    qkv_ref[...] = (mm(tok_ref[...], w_ref[...]) + b_ref[...]).astype(bf16)
    low_half = iota((rows, 128), 1) < hdim
    for p in range(heads // 2):
        k_pair = qkv_ref[:, width + 128 * p : width + 128 * (p + 1)]
        v_t = qkv_ref[:, 2 * width + 128 * p : 2 * width + 128 * (p + 1)].T
        for j in range(2):
            h = 2 * p + j
            logits = factor * mm(k_pair, head_map(map_ref, h)) - (0.5 * factor * factor) * key_offset(k_pair, low_half, j)
            feats = jnp.exp(logits).astype(bf16)
            lhs = masked_rows(v_t[j * hdim : (j + 1) * hdim, :], masks, tail)
            acc_ref[h] += mm(lhs, feats)

    @pl.when(step == pl.num_programs(0) - 1)
    def _():
        emit_states(acc_ref, own_ref, tot_ref, span_ref, send_ref, here, nseg, heads, hdim)


def norm_backward(incoming, scaled, inverse, gain):
    weighted = incoming * gain
    return inverse * (
        weighted
        - jnp.mean(weighted, axis=-1, keepdims=True)
        - scaled * jnp.mean(weighted * scaled, axis=-1, keepdims=True)
    )


def norm_parts(values):
    centred = values - jnp.mean(values, axis=-1, keepdims=True)
    spread = jnp.mean(centred * centred, axis=-1, keepdims=True)
    inverse = lax.rsqrt(spread + norm_epsilon)
    return centred * inverse, inverse


def gelu_parts(u):
    bell = jnp.exp(-0.5 * (u * u))
    t = 1.0 / (1.0 + (0.3275911 * root_half) * jnp.abs(u))
    poly = 0.5 * 1.061405429
    for c in (-1.453152027, 1.421413741, -0.284496736, 0.254829592):
        poly = poly * t + 0.5 * c
    tail = poly * t * bell
    cdf = jnp.where(u < 0.0, tail, 1.0 - tail)
    return u * cdf, cdf + u * (inv_root_tau * bell)


def chain(
    len_ref, tok_ref, q_ref, map_ref, own_ref, tot_ref, span_ref, recv_ref, wo_ref, bo_ref, g1_ref, s1_ref,
    wup_ref, bup_ref, wdn_ref, bdn_ref, g2_ref, s2_ref, cot_ref,
    out_ref, normed_ref, act_ref, bgrad_ref, ugrad_ref, agrad_ref, mixed_ref, num_ref, dgm_ref,
    st_ref, totp_ref, sown_ref, stot_ref, sspan_ref, ssend_ref, vec_ref,
    qf_ref, slope_ref, acc_ref,
    *, half, nseg, heads, hdim, chunk
):
    step = pl.program_id(0)
    rows, width = tok_ref.shape
    feat = map_ref.shape[2]
    wide = nseg * hdim
    starts, ends = bounds(len_ref, nseg)
    here = spanning(ends, half)
    first = lax.axis_index("head") * half + step * rows
    factor = hdim ** (-0.25)

    @pl.when(step == 0)
    def _():
        acc_ref[...] = jnp.zeros_like(acc_ref)
        vec_ref[...] = jnp.zeros_like(vec_ref)
        put_states(own_ref, tot_ref, span_ref, recv_ref, st_ref, totp_ref, here, nseg, heads, hdim)

    pos = first + iota((rows, wide), 0)
    seg_wide = inside(pos, iota((rows, wide), 1) // hdim, starts, ends)
    lane8 = iota((rows, 128), 1) % 8
    pos8 = first + iota((rows, 128), 0)
    seg8 = jnp.logical_and(lane8 < nseg, inside(pos8, lane8, starts, ends))
    total_end = ends[-1]
    low_half = iota((rows, 128), 1) < hdim

    nums = []
    den_c = jnp.zeros((rows, 128), f32)
    for p in range(heads // 2):
        q_pair = q_ref[:, 128 * p : 128 * (p + 1)]
        folded = []
        for j in range(2):
            h = 2 * p + j
            proj = mm(q_pair, head_map(map_ref, h))
            feats = jnp.exp(factor * (proj - jnp.max(proj, axis=-1, keepdims=True))).astype(bf16)
            qf_ref[:, feat * h : feat * (h + 1)] = feats
            den_c += mm_nt(feats, totp_ref[128 * h : 128 * (h + 1), :])
            r = jnp.where(seg_wide, mm_nt(feats, st_ref[wide * h : wide * (h + 1), :]), 0.0)
            folded.append(r[:, :128] + r[:, 128:])
        straight = jnp.where(low_half, folded[0], folded[1])
        crossed = jnp.where(low_half, folded[1], folded[0])
        nums.append(straight + pltpu.roll(crossed, hdim, 1))
    numer = jnp.concatenate(nums, axis=1)
    den_parts = split_hi_lo(jnp.where(seg8, den_c, 0.0))
    row_h = (iota((256, width), 0) % 128) // 8
    expand = as_bf(row_h == iota((256, width), 1) // hdim)
    same8 = as_bf((iota((256, 128), 0) % 128) // 8 == iota((256, 128), 1) // 8)
    dead = jnp.where(first + iota((rows, 128), 0) < total_end, 0.0, 1.0)
    spare = jnp.where(iota((rows, 128), 1) < 8 * heads, dead, 1.0)
    inv_c = 1.0 / (mm(den_parts, same8) + spare)
    den_w = mm(den_parts, expand) + jnp.concatenate([dead] * (width // 128), axis=1)
    inv_w = 1.0 / den_w
    ratio = numer * inv_w
    mixed = ratio.astype(bf16)
    mixed_ref[...] = mixed

    hidden = tok_ref[...].astype(f32) + mm_nt(mixed, wo_ref[...]) + bo_ref[...]
    scaled1, inverse1 = norm_parts(hidden)
    normed = scaled1 * g1_ref[...] + s1_ref[...]
    normed_bf = normed.astype(bf16)
    normed_ref[...] = normed_bf
    branch = jnp.zeros((rows, width), f32)
    hidden_units = wup_ref.shape[1]
    for c in range(hidden_units // chunk):
        cols = slice(c * chunk, (c + 1) * chunk)
        up = mm(normed_bf, wup_ref[:, cols]) + bup_ref[:, cols]
        act, slope = gelu_parts(up)
        act = act.astype(bf16)
        act_ref[:, cols] = act
        slope_ref[:, cols] = slope
        branch += mm_nt(act, wdn_ref[:, cols])
    final = normed + branch + bdn_ref[...]
    scaled2, inverse2 = norm_parts(final)
    out_ref[...] = (scaled2 * g2_ref[...] + s2_ref[...]).astype(bf16)
    incoming = cot_ref[...].astype(f32)
    grad_final = norm_backward(incoming, scaled2, inverse2, g2_ref[...])
    bgrad = grad_final.astype(bf16)
    bgrad_ref[...] = bgrad

    def add_row(row, values):
        vec_ref[row : row + 1, :] += jnp.sum(values, axis=0, keepdims=True)

    add_row(3, grad_final)
    add_row(4, incoming * scaled2)
    add_row(5, incoming)
    back = jnp.zeros((rows, width), f32)
    for c in range(hidden_units // chunk):
        cols = slice(c * chunk, (c + 1) * chunk)
        ugrad = (mm(bgrad, wdn_ref[:, cols]) * slope_ref[:, cols]).astype(bf16)
        ugrad_ref[:, cols] = ugrad
        sums = jnp.sum(ugrad.astype(f32), axis=0, keepdims=True)
        for k in range(chunk // width):
            row = 6 + (c * chunk) // width + k
            vec_ref[row : row + 1, :] += sums[:, k * width : (k + 1) * width]
        back += mm_nt(ugrad, wup_ref[:, cols])
    grad_normed = grad_final + back
    grad_hidden = norm_backward(grad_normed, scaled1, inverse1, g1_ref[...])
    add_row(0, grad_hidden)
    add_row(1, grad_normed * scaled1)
    add_row(2, grad_normed)
    agrad = grad_hidden.astype(bf16)
    agrad_ref[...] = agrad

    grad_mixed = mm(agrad, wo_ref[...])
    num_grad = (grad_mixed * inv_w).astype(bf16)
    num_ref[...] = num_grad
    inner = split_hi_lo(grad_mixed * ratio)
    gather = as_bf((iota((2 * width, 128), 0) % width) // hdim == iota((2 * width, 128), 1) // 8)
    den_grad = -(mm(inner, gather) * inv_c)
    den_m = jnp.where(seg8, den_grad, 0.0).astype(bf16)
    dgm_ref[...] = den_m
    den_t = den_m.T
    masks, _ = lane_segment_masks(first, rows, hdim, starts, ends)
    pad = jnp.zeros((8, rows), bf16)
    for p in range(heads // 2):
        num_t = num_grad[:, 128 * p : 128 * (p + 1)].T
        tails = den_t[16 * p : 16 * p + 16, :]
        for j in range(2):
            h = 2 * p + j
            tail = jnp.concatenate([tails[8 * j : 8 * j + 8, :], pad], axis=0)
            lhs = masked_rows(num_t[j * hdim : (j + 1) * hdim, :], masks, tail)
            acc_ref[h] += mm(lhs, qf_ref[:, feat * h : feat * (h + 1)])

    @pl.when(step == pl.num_programs(0) - 1)
    def _():
        emit_states(acc_ref, sown_ref, stot_ref, sspan_ref, ssend_ref, here, nseg, heads, hdim)


def replicate(pair, low_half, hdim):
    wide = pair.astype(f32)
    other = pltpu.roll(wide, hdim, 1)
    return (jnp.where(low_half, wide, other).astype(bf16), jnp.where(low_half, other, wide).astype(bf16))


def attention_back(
    len_ref, qkv_ref, num_ref, dgm_ref, map_ref, st_ref, totp_ref, sown_ref, stot_ref, sspan_ref, srecv_ref,
    pg_ref, vec_ref, sg_ref, sgt_ref, mapg_ref,
    *, half, nseg, heads, hdim, width
):
    step = pl.program_id(0)
    rows = qkv_ref.shape[0]
    feat = map_ref.shape[2]
    wide = nseg * hdim
    starts, ends = bounds(len_ref, nseg)
    here = spanning(ends, half)
    first = lax.axis_index("head") * half + step * rows
    factor = hdim ** (-0.25)

    @pl.when(step == 0)
    def _():
        vec_ref[...] = jnp.zeros_like(vec_ref)
        put_states(sown_ref, stot_ref, sspan_ref, srecv_ref, sg_ref, sgt_ref, here, nseg, heads, hdim)
        one, zero = jnp.ones((hdim, feat), bf16), jnp.zeros((hdim, feat), bf16)
        for p in range(heads // 2):
            left = jnp.concatenate([map_ref[2 * p], zero, one, zero], axis=0)
            right = jnp.concatenate([zero, map_ref[2 * p + 1], zero, one], axis=0)
            mapg_ref[p] = jnp.concatenate([left, right], axis=1)

    pos = first + iota((rows, wide), 0)
    seg_wide = inside(pos, iota((rows, wide), 1) // hdim, starts, ends)
    seg_wide_bf = as_bf(seg_wide)
    lane8 = iota((rows, 128), 1) % 8
    pos8 = first + iota((rows, 128), 0)
    seg8_bf = as_bf(jnp.logical_and(lane8 < nseg, inside(pos8, lane8, starts, ends)))
    low_half = iota((rows, 128), 1) < hdim
    den_m = dgm_ref[...]

    for p in range(heads // 2):
        q_pair = qkv_ref[:, 128 * p : 128 * (p + 1)]
        k_pair = qkv_ref[:, width + 128 * p : width + 128 * (p + 1)]
        v_pair = qkv_ref[:, 2 * width + 128 * p : 2 * width + 128 * (p + 1)]
        num_reps = replicate(num_ref[:, 128 * p : 128 * (p + 1)], low_half, hdim)
        v_reps = replicate(v_pair, low_half, hdim)
        q_logs, k_logs, folded = [], [], []
        for j in range(2):
            h = 2 * p + j
            own_map = head_map(map_ref, h)
            proj = mm(q_pair, own_map)
            shifted = proj - jnp.max(proj, axis=-1, keepdims=True)
            lhs = jnp.concatenate([num_reps[j]] * 2, axis=1) * seg_wide_bf
            q_slope = mm(lhs, st_ref[wide * h : wide * (h + 1), :]) + mm(den_m, totp_ref[128 * h : 128 * (h + 1), :])
            q_slope = q_slope * jnp.exp(factor * shifted)
            peak = jnp.where(shifted == 0.0, 1.0, 0.0)
            share = jnp.sum(q_slope, axis=-1, keepdims=True) / jnp.sum(peak, axis=-1, keepdims=True)
            q_logs.append((q_slope - peak * share).astype(bf16))

            logits = factor * mm(k_pair, own_map) - (0.5 * factor * factor) * key_offset(k_pair, low_half, j)
            k_exp = jnp.exp(logits)
            lhs = jnp.concatenate([v_reps[j]] * 2, axis=1) * seg_wide_bf
            state_grad = sg_ref[wide * h : wide * (h + 1), :]
            k_slope = mm(lhs, state_grad) + mm(seg8_bf, sgt_ref[128 * h : 128 * (h + 1), :])
            k_logs.append((k_slope * k_exp).astype(bf16))
            r = jnp.where(seg_wide, mm_nt(k_exp.astype(bf16), state_grad), 0.0)
            folded.append(r[:, :128] + r[:, 128:])
        straight = jnp.where(low_half, folded[0], folded[1])
        crossed = jnp.where(low_half, folded[1], folded[0])
        v_grad = (straight + pltpu.roll(crossed, hdim, 1)).astype(bf16)
        for at, rows_bf, logs in ((0, q_pair, q_logs), (1, k_pair, k_logs)):
            r = mm_nt(jnp.concatenate(logs, axis=1), mapg_ref[p])
            grad = factor * r[:, :128] - (factor * factor) * rows_bf.astype(f32) * r[:, 128:]
            pg_ref[:, at * width + 128 * p : at * width + 128 * (p + 1)] = grad.astype(bf16)
        pg_ref[:, 2 * width + 128 * p : 2 * width + 128 * (p + 1)] = v_grad
    for at in range(3):
        grads = pg_ref[:, at * width : (at + 1) * width].astype(f32)
        vec_ref[at : at + 1, :] += jnp.sum(grads, axis=0, keepdims=True)


def weight_grads(normed_ref, bgrad_ref, agrad_ref, ugrad_ref, act_ref, mixed_ref, dup_ref, ddn_ref, dout_ref, nt_ref, bt_ref, at_ref):
    @pl.when(pl.program_id(0) == 0)
    def _():
        nt_ref[...] = normed_ref[...].T
        bt_ref[...] = bgrad_ref[...].T
        at_ref[...] = agrad_ref[...].T

    ddn_ref[...] = mm(bt_ref[...], act_ref[...]).astype(bf16)
    dup_ref[...] = mm(nt_ref[...], ugrad_ref[...]).astype(bf16)
    dout_ref[...] = mm(at_ref[...], mixed_ref[...]).astype(bf16)


def qkv_weight_grads(tok_ref, pg_ref, dw_ref, tt_ref):
    @pl.when(pl.program_id(0) == 0)
    def _():
        tt_ref[...] = tok_ref[...].T

    dw_ref[...] = mm(tt_ref[...], pg_ref[...]).astype(bf16)


def params(flops=0, moved=0):
    return dict(
        compiler_params=pltpu.CompilerParams(vmem_limit_bytes=vmem_limit),
        cost_estimate=pl.CostEstimate(flops=int(flops), bytes_accessed=int(moved), transcendentals=0),
    )


def whole(shape):
    return pl.BlockSpec(shape, lambda i: (0,) * len(shape), pipeline_mode=pl.Buffered(1))


def resident(shape):
    return pl.BlockSpec(shape, lambda i: (0,) * len(shape))


def sds(shape, dtype):
    return jax.ShapeDtypeStruct(shape, dtype)


def reduce_scatter(grad, dp_count, order):
    bits = dp_count.bit_length() - 1
    row_count = grad.shape[0] // dp_count
    left = list(range(bits - 1, -1, -1))
    me = lax.axis_index("dp")
    x = lax.axis_index("head")
    part = grad.reshape((2,) * bits + (row_count, grad.shape[1]))
    for n, stage in enumerate(order):
        if stage == "x":
            axis, pairs, mine = "head", [(0, 1), (1, 0)], x
            half = part.shape[-1] // 2
            send = lax.dynamic_slice_in_dim(part, (1 - x) * half, half, axis=part.ndim - 1)
            keep = lax.dynamic_slice_in_dim(part, x * half, half, axis=part.ndim - 1)
        else:
            axis, pairs = "dp", [(i, i ^ (1 << stage)) for i in range(dp_count)]
            mine = (me >> stage) & 1
            dim = left.index(stage)
            left.remove(stage)
            send = lax.dynamic_index_in_dim(part, 1 - mine, dim, keepdims=False)
            keep = lax.dynamic_index_in_dim(part, mine, dim, keepdims=False)
        got = lax.ppermute(send, axis, pairs)
        part = keep.astype(f32) + got.astype(f32)
        if n < len(order) - 1:
            part = part.astype(bf16)
    return part


def sum_all(values, dp_count):
    for stage in ["x"] + list(range(dp_count.bit_length() - 1)):
        if stage == "x":
            got = lax.ppermute(values, "head", [(0, 1), (1, 0)])
        else:
            got = lax.ppermute(values, "dp", [(i, i ^ (1 << stage)) for i in range(dp_count)])
        values = values + got
    return values


def body(
    tokens, lengths, feature_map, qkv_weight, qkv_bias, out_weight, out_bias, ln1_gain, ln1_shift,
    up_weight, up_bias, down_weight, down_bias, ln2_gain, ln2_shift, cotangent,
):
    half, width = tokens.shape
    heads, hdim, feat = feature_map.shape
    nseg = lengths.shape[1]
    hidden_units = up_weight.shape[1]
    wide = nseg * hdim
    dp_count = lax.axis_size("dp")
    head_count = lax.axis_size("head")
    bits = dp_count.bit_length() - 1
    assert head_count == 2 and dp_count == 1 << bits and 2 * hdim == 128 and wide == 256 and 8 * heads <= 128
    flat_w = qkv_weight.reshape(width, 3 * width)
    flat_b = qkv_bias.reshape(1, 3 * width)
    rows = min(256, half)
    steps = half // rows
    span_rows = heads * hdim + 16
    state_shapes = [
        sds((heads * wide, feat), bf16), sds((heads * 8, feat), f32),
        sds((span_rows - 16, feat), f32), sds((span_rows, feat), bf16),
    ]
    state_specs = [resident(s.shape) for s in state_shapes]
    lens = pl.BlockSpec(memory_space=pltpu.SMEM)

    def tile(cols, col=0):
        return pl.BlockSpec((rows, cols), lambda i: (i, col))

    static = dict(half=half, nseg=nseg, heads=heads, hdim=hdim)
    dense = 2 * half * width

    qkv, own, tot, span, send = pl.pallas_call(
        functools.partial(forward_keys, width=width, **static),
        grid=(steps,),
        in_specs=[lens, tile(width), whole(flat_w.shape), whole(flat_b.shape), whole(feature_map.shape)],
        out_specs=[tile(3 * width)] + state_specs,
        out_shape=[sds((half, 3 * width), bf16)] + state_shapes,
        scratch_shapes=[pltpu.VMEM((heads, wide + 16, feat), f32)],
        **params(dense * 3 * width, 16e6),
    )(lengths, tokens, flat_w, flat_b, feature_map)
    recv = lax.ppermute(send, "head", [(0, 1), (1, 0)])

    row = lambda v: v.reshape(1, -1)
    vec_rows = 6 + hidden_units // width
    vec_rows += -vec_rows % 8
    chunk = width
    (output, normed, act, bgrad, ugrad, agrad, mixed, num_grad, den_m, states, totals, s_own, s_tot, s_span, s_send, vec_b) = pl.pallas_call(
        functools.partial(chain, chunk=chunk, **static),
        grid=(steps,),
        in_specs=[lens, tile(width), tile(width), whole(feature_map.shape)]
        + [whole(v.shape) for v in (own, tot, span, recv)]
        + [whole(out_weight.shape), whole((1, width)), whole((1, width)), whole((1, width))]
        + [whole(up_weight.shape), whole((1, hidden_units)), whole(down_weight.shape)]
        + [whole((1, width))] * 3
        + [tile(width)],
        out_specs=[tile(width), tile(width), tile(hidden_units), tile(width), tile(hidden_units), tile(width), tile(width), tile(width), tile(128)]
        + [resident((heads * wide, feat)), resident((heads * 128, feat))]
        + state_specs
        + [resident((vec_rows, width))],
        out_shape=[sds((half, c), bf16) for c in (width, width, hidden_units, width, hidden_units, width, width, width, 128)]
        + [sds((heads * wide, feat), bf16), sds((heads * 128, feat), bf16)]
        + state_shapes
        + [sds((vec_rows, width), f32)],
        scratch_shapes=[
            pltpu.VMEM((rows, heads * feat), bf16),
            pltpu.VMEM((rows, hidden_units), f32),
            pltpu.VMEM((heads, wide + 16, feat), f32),
        ],
        **params(dense * (4 * hidden_units + 4 * width), 40e6),
    )(
        lengths, tokens, qkv, feature_map, own, tot, span, recv, out_weight, row(out_bias), row(ln1_gain), row(ln1_shift),
        up_weight, row(up_bias), down_weight, row(down_bias), row(ln2_gain), row(ln2_shift), cotangent,
    )
    s_recv = lax.ppermute(s_send, "head", [(0, 1), (1, 0)])

    cols = 512
    parts = hidden_units // cols
    out_cols = width // parts
    col_tile = lambda r, c: pl.BlockSpec((r, c), lambda i: (0, i))
    d_up, d_down, d_out = pl.pallas_call(
        weight_grads,
        grid=(parts,),
        in_specs=[whole((half, width))] * 3 + [col_tile(half, cols), col_tile(half, cols), col_tile(half, out_cols)],
        out_specs=[col_tile(width, cols), col_tile(width, cols), col_tile(width, out_cols)],
        out_shape=[sds((width, hidden_units), bf16), sds((width, hidden_units), bf16), sds((width, width), bf16)],
        scratch_shapes=[pltpu.VMEM((width, half), bf16)] * 3,
        **params(dense * (2 * hidden_units + width), 30e6),
    )(normed, bgrad, agrad, ugrad, act, mixed)

    proj_grad, vec_c = pl.pallas_call(
        functools.partial(attention_back, width=width, **static),
        grid=(steps,),
        in_specs=[lens, tile(3 * width), tile(width), tile(128), whole(feature_map.shape)]
        + [whole(v.shape) for v in (states, totals, s_own, s_tot, s_span, s_recv)],
        out_specs=[tile(3 * width), resident((8, width))],
        out_shape=[sds((half, 3 * width), bf16), sds((8, width), f32)],
        scratch_shapes=[
            pltpu.VMEM((heads * wide, feat), bf16),
            pltpu.VMEM((heads * 128, feat), bf16),
            pltpu.VMEM((heads // 2, 4 * hdim, 2 * feat), bf16),
        ],
        **params(dense * 3 * width, 16e6),
    )(lengths, qkv, num_grad, den_m, feature_map, states, totals, s_own, s_tot, s_span, s_recv)

    half_w = width // 2
    d_qkv = pl.pallas_call(
        qkv_weight_grads,
        grid=(6,),
        in_specs=[whole((half, width)), col_tile(half, half_w)],
        out_specs=pl.BlockSpec((width, half_w), lambda i: (0, (i % 2) * 3 + i // 2)),
        out_shape=sds((width, 3 * width), bf16),
        scratch_shapes=[pltpu.VMEM((width, half), bf16)],
        **params(dense * 3 * width, 10e6),
    )(tokens, proj_grad)
    grad_tokens = (agrad.astype(f32) + mm_nt(proj_grad, flat_w)).astype(bf16)

    upper = list(range(2, bits))
    order_a = [0, "x", 1] + upper
    order_b = [0, 1, "x"] + upper
    d_down = reduce_scatter(d_down, dp_count, order_a)
    d_up = reduce_scatter(d_up, dp_count, order_b)
    d_out = reduce_scatter(d_out, dp_count, order_a)
    d_qkv = reduce_scatter(d_qkv, dp_count, order_b)
    vectors = sum_all(jnp.concatenate([vec_b, vec_c], axis=0), dp_count)
    up_rows = hidden_units // width
    return (
        output,
        grad_tokens,
        d_qkv.reshape(-1, 3, half_w),
        vectors[vec_rows : vec_rows + 3],
        d_out,
        vectors[0],
        vectors[1],
        vectors[2],
        d_up,
        vectors[6 : 6 + up_rows].reshape(-1),
        d_down,
        vectors[3],
        vectors[4],
        vectors[5],
    )


def solution(mesh):
    rows = P(("dp", "head"), None)
    in_specs = (rows, P("dp", None)) + (P(),) * 13 + (rows,)
    out_specs = (
        rows, rows, P("dp", None, "head"), P(), P("dp", "head"), P(), P(), P(),
        P("dp", "head"), P(), P("dp", "head"), P(), P(), P(),
    )
    return jax.shard_map(body, mesh=mesh, in_specs=in_specs, out_specs=out_specs, check_vma=False)
```

```python
import functools

import jax
import jax.numpy as jnp
from jax import lax
from jax.experimental import pallas as pl
from jax.experimental.pallas import tpu as pltpu
from jax.sharding import PartitionSpec as P

bf16 = jnp.bfloat16
f32 = jnp.float32
norm_epsilon = 1e-06
root_half = 0.7071067811865476
inv_root_tau = 0.3989422804014327
vmem_limit = 60 * 1024 * 1024
nt_dims = (((1,), (1,)), ((), ()))


def mm(a, b):
    return jnp.dot(a, b, preferred_element_type=f32)


def mm_nt(a, b):
    return lax.dot_general(a, b, nt_dims, preferred_element_type=f32)


def iota(shape, dim):
    return lax.broadcasted_iota(jnp.int32, shape, dim)


def bounds(len_ref, nseg):
    starts, ends, run = [], [], jnp.int32(0)
    for s in range(nseg):
        starts.append(run)
        run = run + len_ref[0, s]
        ends.append(run)
    return starts, ends


def spanning(ends, half):
    count = jnp.int32(0)
    for end in ends:
        count = count + (end < half).astype(jnp.int32)
    return count


def pick(index, values):
    out = jnp.full(index.shape, values[-1], jnp.int32)
    for s in range(len(values) - 2, -1, -1):
        out = jnp.where(index == s, values[s], out)
    return out


def inside(pos, index, starts, ends):
    return jnp.logical_and(pos >= pick(index, starts), pos < pick(index, ends))


def as_bf(mask):
    return jnp.where(mask, 1.0, 0.0).astype(bf16)


def split_hi_lo(v):
    hi = v.astype(bf16)
    lo = (v - hi.astype(f32)).astype(bf16)
    return jnp.concatenate([hi, lo], axis=1)


def masked_rows(rows_t, lane_masks, tail):
    return jnp.concatenate([rows_t * m for m in lane_masks] + [tail], axis=0)


def head_map(map_ref, h):
    m = map_ref[h]
    z = jnp.zeros_like(m)
    return jnp.concatenate([m, z] if h % 2 == 0 else [z, m], axis=0)


def key_offset(k_pair, low_half, j):
    sq = jnp.square(k_pair.astype(f32))
    mine = low_half if j == 0 else jnp.logical_not(low_half)
    return jnp.sum(jnp.where(mine, sq, 0.0), axis=-1, keepdims=True)


def put_states(own_ref, tot_ref, span_ref, recv_ref, st_ref, totp_ref, here, nseg, heads, hdim):
    wide = nseg * hdim
    feat = st_ref.shape[1]
    recv_tot = recv_ref[heads * hdim :, :].astype(f32)
    seg_row = iota((8, feat), 0)
    for h in range(heads):
        st_ref[h * wide : (h + 1) * wide, :] = own_ref[h * wide : (h + 1) * wide, :]
        both = span_ref[h * hdim : (h + 1) * hdim, :] + recv_ref[h * hdim : (h + 1) * hdim, :].astype(f32)
        at = pl.multiple_of(h * wide + here * hdim, hdim)
        st_ref[pl.ds(at, hdim), :] = both.astype(bf16)
        tot = tot_ref[8 * h : 8 * h + 8, :]
        tot = jnp.where(seg_row == here, tot + recv_tot[h : h + 1, :], tot)
        parts = [tot]
        if h > 0:
            parts.insert(0, jnp.zeros((8 * h, feat), f32))
        if 8 * h + 8 < 128:
            parts.append(jnp.zeros((128 - 8 * h - 8, feat), f32))
        totp_ref[:, feat * h : feat * (h + 1)] = jnp.concatenate(parts, axis=0).astype(bf16)


def emit_states(acc_ref, own_ref, tot_ref, span_ref, send_ref, here, nseg, heads, hdim):
    wide = nseg * hdim
    feat = acc_ref.shape[2]
    for h in range(heads):
        own_ref[h * wide : (h + 1) * wide, :] = acc_ref[h, 0:wide, :].astype(bf16)
        tot_ref[8 * h : 8 * h + 8, :] = acc_ref[h, wide : wide + 8, :]
        at = pl.multiple_of(here * hdim, hdim)
        part = acc_ref[h, pl.ds(at, hdim), :]
        span_ref[h * hdim : (h + 1) * hdim, :] = part
        send_ref[h * hdim : (h + 1) * hdim, :] = part.astype(bf16)
    row = iota((16, feat), 0)
    seg_row = iota((8, feat), 0)
    tots = jnp.zeros((16, feat), f32)
    for h in range(heads):
        mine = jnp.sum(jnp.where(seg_row == here, acc_ref[h, wide : wide + 8, :], 0.0), axis=0, keepdims=True)
        tots = jnp.where(row == h, mine, tots)
    send_ref[heads * hdim :, :] = tots.astype(bf16)


def lane_segment_masks(first, rows, hdim, starts, ends):
    pos = first + iota((hdim, rows), 1)
    masks = [as_bf(jnp.logical_and(pos >= a, pos < b)) for a, b in zip(starts, ends)]
    pos = first + iota((16, rows), 1)
    seg = iota((16, rows), 0)
    tail = as_bf(jnp.logical_and(seg < len(starts), inside(pos, seg, starts, ends)))
    return masks, tail


def seg_masks(first, rows, hdim, nseg, starts, ends):
    pos = first + iota((rows, nseg * hdim), 0)
    wide = inside(pos, iota((rows, nseg * hdim), 1) // hdim, starts, ends)
    lane8 = iota((rows, 128), 1) % 8
    pos = first + iota((rows, 128), 0)
    eight = jnp.logical_and(lane8 < nseg, inside(pos, lane8, starts, ends))
    return wide, eight


def block_of(p, dp_count):
    top = dp_count.bit_length() - 1
    return (p >> (top - 1)) & 1 | ((p >> (top - 2)) & 1) << 1 | (p & (dp_count // 4 - 1)) << 2


def dp_index():
    return (lax.axis_index("z") * 2 + lax.axis_index("y")) * 2 + lax.axis_index("c")


def row_sources(dp_count):
    return [jnp.bitwise_xor(dp_index(), block_of(p, dp_count)) for p in range(dp_count)]


def put_transposed(lhs_ref, tmp_ref, values, at, sources):
    rows, width = values.shape
    cols = pl.ds(at, rows)
    if not sources:
        lhs_ref[:, cols] = values.T
        return
    block = width // len(sources)
    tmp_ref[...] = values.T
    for p, source in enumerate(sources):
        lhs_ref[p * block : (p + 1) * block, cols] = tmp_ref[pl.ds(pl.multiple_of(source * block, 16), block), :]


def fold_pair(folded, low_half, hdim):
    straight = jnp.where(low_half, folded[0], folded[1])
    crossed = jnp.where(low_half, folded[1], folded[0])
    return straight + pltpu.roll(crossed, hdim, 1)


def forward_keys(
    len_ref, tok_ref, wk_ref, wv_ref, b_ref, map_ref, kv_ref, own_ref, tot_ref, span_ref, send_ref, acc_ref,
    *, half, nseg, heads, hdim
):
    step = pl.program_id(0)
    rows, width = tok_ref.shape
    starts, ends = bounds(len_ref, nseg)
    here = spanning(ends, half)
    first = lax.axis_index("x") * half + step * rows
    factor = hdim ** (-0.25)

    @pl.when(step == 0)
    def _():
        acc_ref[...] = jnp.zeros_like(acc_ref)

    masks, tail = lane_segment_masks(first, rows, hdim, starts, ends)
    tok = tok_ref[...]
    keys = (mm(tok, wk_ref[...]) + b_ref[1:2, :]).astype(bf16)
    vals = (mm(tok, wv_ref[...]) + b_ref[2:3, :]).astype(bf16)
    kv_ref[:, :width] = keys
    kv_ref[:, width:] = vals
    low_half = iota((rows, 128), 1) < hdim
    for p in range(heads // 2):
        k_pair = keys[:, 128 * p : 128 * (p + 1)]
        v_t = vals[:, 128 * p : 128 * (p + 1)].T
        for j in range(2):
            h = 2 * p + j
            logits = factor * mm(k_pair, head_map(map_ref, h)) - (0.5 * factor * factor) * key_offset(k_pair, low_half, j)
            feats = jnp.exp(logits).astype(bf16)
            lhs = masked_rows(v_t[j * hdim : (j + 1) * hdim, :], masks, tail)
            acc_ref[h] += mm(lhs, feats)

    @pl.when(step == pl.num_programs(0) - 1)
    def _():
        emit_states(acc_ref, own_ref, tot_ref, span_ref, send_ref, here, nseg, heads, hdim)


def forward_queries(tok_ref, wq_ref, b_ref, map_ref, q_ref, qf_ref, *, heads, hdim):
    feat = map_ref.shape[2]
    factor = hdim ** (-0.25)
    queries = (mm(tok_ref[...], wq_ref[...]) + b_ref[0:1, :]).astype(bf16)
    q_ref[...] = queries
    for h in range(heads):
        proj = mm(queries[:, 128 * (h // 2) : 128 * (h // 2 + 1)], head_map(map_ref, h))
        top = jnp.max(proj, axis=-1, keepdims=True)
        qf_ref[:, feat * h : feat * (h + 1)] = jnp.exp(factor * (proj - top)).astype(bf16)


def norm_backward(incoming, scaled, inverse, gain):
    weighted = incoming * gain
    return inverse * (
        weighted
        - jnp.mean(weighted, axis=-1, keepdims=True)
        - scaled * jnp.mean(weighted * scaled, axis=-1, keepdims=True)
    )


def norm_parts(values):
    centred = values - jnp.mean(values, axis=-1, keepdims=True)
    spread = jnp.mean(centred * centred, axis=-1, keepdims=True)
    inverse = lax.rsqrt(spread + norm_epsilon)
    return centred * inverse, inverse


def gelu_parts(u):
    cdf = 0.5 + 0.5 * lax.erf(u * root_half)
    return u * cdf, cdf + u * (inv_root_tau * jnp.exp(-0.5 * (u * u)))


def flat_row(ref):
    return ref[...].reshape(1, -1)


def add_row(vec_ref, row, values):
    vec_ref[row : row + 1, :] += jnp.sum(values, axis=0, keepdims=True)


def put_grad(keep_ref, send_ref, grad):
    quarter = grad.shape[0] // 4
    for b in range(grad.shape[1] // 128):
        cols = slice(128 * b, 128 * (b + 1))
        for y in range(2):
            keep_ref[y, 0, b] = grad[y * quarter : (y + 1) * quarter, cols].astype(bf16)
            send_ref[y, 0, b] = grad[(2 + y) * quarter : (3 + y) * quarter, cols].astype(bf16)


def half_cols(xr, half_width):
    x = lax.axis_index("x")
    return pl.multiple_of(jnp.bitwise_xor(x, xr) * half_width, 128)


def chain(
    len_ref, tok_ref, qf_ref, cot_ref, own_ref, tot_ref, span_ref, recv_ref, wo_ref, bo_ref, g1_ref, s1_ref,
    wup_hbm, bup_ref, wdn_hbm, bdn_ref, g2_ref, s2_ref,
    out_ref, agrad_ref, num_ref, dgm_ref, vec_ref, sown_ref, stot_ref, sspan_ref, ssend_ref,
    dkeep_ref, dsend_ref, ukeep_ref, usend_ref, okeep_ref, osend_ref,
    st_ref, totp_ref, acc_ref, act_ref, up_ref, mix_ref, slope_ref, dlhs_ref, ulhs_ref, olhs_ref, tmp_ref, wup_ref, wdn_ref, sem,
    *, half, nseg, heads, hdim, chunk, steps, dp_count, sort
):
    step = pl.program_id(0)
    rows, width = tok_ref.shape
    wide = nseg * hdim
    feat = st_ref.shape[1]
    hidden_units = wup_ref.shape[1]
    starts, ends = bounds(len_ref, nseg)
    here = spanning(ends, half)
    first = lax.axis_index("x") * half + step * rows
    fetch = [pltpu.make_async_copy(wup_hbm, wup_ref, sem.at[0]), pltpu.make_async_copy(wdn_hbm, wdn_ref, sem.at[1])]

    @pl.when(step == 0)
    def _():
        fetch[0].start()
        fetch[1].start()
        vec_ref[...] = jnp.zeros_like(vec_ref)
        acc_ref[...] = jnp.zeros_like(acc_ref)
        put_states(own_ref, tot_ref, span_ref, recv_ref, st_ref, totp_ref, here, nseg, heads, hdim)

    @pl.when(step < steps)
    def _():
        at = pl.multiple_of(step * rows, 128)
        mine = pl.ds(at, rows)
        seg_wide, seg8 = seg_masks(first, rows, hdim, nseg, starts, ends)
        low_half = iota((rows, 128), 1) < hdim
        nums = []
        for p in range(heads // 2):
            folded = []
            for j in range(2):
                h = 2 * p + j
                r = mm_nt(qf_ref[:, feat * h : feat * (h + 1)], st_ref[wide * h : wide * (h + 1), :])
                r = jnp.where(seg_wide, r, 0.0)
                folded.append(r[:, :128] + r[:, 128:])
            nums.append(fold_pair(folded, low_half, hdim))
        numer = jnp.concatenate(nums, axis=1)
        den_parts = split_hi_lo(jnp.where(seg8, mm_nt(qf_ref[...], totp_ref[...]), 0.0))
        expand = as_bf((iota((256, width), 0) % 128) // 8 == iota((256, width), 1) // hdim)
        same8 = as_bf((iota((256, 128), 0) % 128) // 8 == iota((256, 128), 1) // 8)
        dead = jnp.where(first + iota((rows, 128), 0) < ends[-1], 0.0, 1.0)
        spare = jnp.where(iota((rows, 128), 1) < 8 * heads, dead, 1.0)
        inv_c = 1.0 / (mm(den_parts, same8) + spare)
        inv_w = 1.0 / (mm(den_parts, expand) + jnp.concatenate([dead] * (width // 128), axis=1))
        ratio = numer * inv_w
        mixed = ratio.astype(bf16)
        mix_ref[mine, :] = mixed

        hidden = tok_ref[...].astype(f32) + mm_nt(mixed, wo_ref[...]) + flat_row(bo_ref)
        scaled1, inverse1 = norm_parts(hidden)
        normed = scaled1 * flat_row(g1_ref) + flat_row(s1_ref)
        normed_bf = normed.astype(bf16)
        put_transposed(ulhs_ref, tmp_ref, normed_bf, at, row_sources(dp_count) if sort else [])

        @pl.when(step == 0)
        def _():
            fetch[0].wait()
            fetch[1].wait()

        count = hidden_units // chunk
        cols = [slice(c * chunk, (c + 1) * chunk) for c in range(count)]
        bup = flat_row(bup_ref)
        up = mm(normed_bf, wup_ref[:, cols[0]]) + bup[:, cols[0]]
        branch = normed + flat_row(bdn_ref)
        last = None
        for c in range(count):
            later = mm(normed_bf, wup_ref[:, cols[c + 1]]) + bup[:, cols[c + 1]] if c + 1 < count else None
            act, slope = gelu_parts(up)
            act = act.astype(bf16)
            act_ref[mine, cols[c]] = act
            slope_ref[:, cols[c]] = slope.astype(slope_ref.dtype)
            if last is not None:
                branch += mm_nt(last, wdn_ref[:, cols[c - 1]])
            last, up = act, later
        final = branch + mm_nt(last, wdn_ref[:, cols[count - 1]])
        scaled2, inverse2 = norm_parts(final)
        gain2 = flat_row(g2_ref)
        out_ref[...] = (scaled2 * gain2 + flat_row(s2_ref)).astype(bf16)
        incoming = cot_ref[...].astype(f32)
        grad_final = norm_backward(incoming, scaled2, inverse2, gain2)
        bgrad = grad_final.astype(bf16)
        add_row(vec_ref, 0, grad_final)
        add_row(vec_ref, 1, incoming * scaled2)
        add_row(vec_ref, 2, incoming)
        put_transposed(dlhs_ref, tmp_ref, bgrad, at, row_sources(dp_count) if sort else [])

        grad_normed = grad_final
        wide_grad = mm(bgrad, wdn_ref[:, cols[0]])
        last = None
        for c in range(count):
            later = mm(bgrad, wdn_ref[:, cols[c + 1]]) if c + 1 < count else None
            ugrad = (wide_grad * slope_ref[:, cols[c]].astype(f32)).astype(bf16)
            up_ref[mine, cols[c]] = ugrad
            sums = jnp.sum(ugrad.astype(f32), axis=0, keepdims=True)
            for k in range(0, chunk, 128):
                row, col = divmod(c * chunk + k, width)
                vec_ref[6 + row : 7 + row, col : col + 128] += sums[:, k : k + 128]
            if last is not None:
                grad_normed += mm_nt(last, wup_ref[:, cols[c - 1]])
            last, wide_grad = ugrad, later
        grad_normed += mm_nt(last, wup_ref[:, cols[count - 1]])

        grad_hidden = norm_backward(grad_normed, scaled1, inverse1, flat_row(g1_ref))
        add_row(vec_ref, 3, grad_hidden)
        add_row(vec_ref, 4, grad_normed * scaled1)
        add_row(vec_ref, 5, grad_normed)
        agrad = grad_hidden.astype(bf16)
        agrad_ref[...] = agrad
        put_transposed(olhs_ref, tmp_ref, agrad, at, row_sources(dp_count) if sort else [])

        grad_mixed = mm(agrad, wo_ref[...])
        num_grad = (grad_mixed * inv_w).astype(bf16)
        num_ref[...] = num_grad
        inner = split_hi_lo(grad_mixed * ratio)
        gather = as_bf((iota((2 * width, 128), 0) % width) // hdim == iota((2 * width, 128), 1) // 8)
        den_m = jnp.where(seg8, -(mm(inner, gather) * inv_c), 0.0).astype(bf16)
        dgm_ref[...] = den_m
        den_t = den_m.T
        masks, _ = lane_segment_masks(first, rows, hdim, starts, ends)
        pad = jnp.zeros((8, rows), bf16)
        for p in range(heads // 2):
            num_t = num_grad[:, 128 * p : 128 * (p + 1)].T
            tails = den_t[16 * p : 16 * p + 16, :]
            for j in range(2):
                h = 2 * p + j
                tail = jnp.concatenate([tails[8 * j : 8 * j + 8, :], pad], axis=0)
                lhs = masked_rows(num_t[j * hdim : (j + 1) * hdim, :], masks, tail)
                acc_ref[h] += mm(lhs, qf_ref[:, feat * h : feat * (h + 1)])

    @pl.when(step == steps - 1)
    def _():
        emit_states(acc_ref, sown_ref, stot_ref, sspan_ref, ssend_ref, here, nseg, heads, hdim)

    own = hidden_units // 2
    count = hidden_units // chunk
    tile = step - steps

    @pl.when(jnp.logical_and(tile >= 0, tile < count))
    def _():
        xr = tile // (count // 2)
        at = half_cols(xr, own) + (tile - xr * (count // 2)) * chunk
        rhs = act_ref[:, pl.ds(pl.multiple_of(at, 128), chunk)]
        put_grad(dkeep_ref, dsend_ref, mm(dlhs_ref[...], rhs))

    @pl.when(jnp.logical_and(tile >= count, tile < 2 * count))
    def _():
        xr = (tile - count) // (count // 2)
        at = half_cols(xr, own) + (tile - count - xr * (count // 2)) * chunk
        put_grad(ukeep_ref, usend_ref, mm(ulhs_ref[...], up_ref[:, pl.ds(pl.multiple_of(at, 128), chunk)]))

    @pl.when(tile >= 2 * count)
    def _():
        rhs = mix_ref[:, pl.ds(half_cols(tile - 2 * count, width // 2), width // 2)]
        put_grad(okeep_ref, osend_ref, mm(olhs_ref[...], rhs))


def replicate(pair, low_half, hdim):
    wide = pair.astype(f32)
    other = pltpu.roll(wide, hdim, 1)
    return (jnp.where(low_half, wide, other).astype(bf16), jnp.where(low_half, other, wide).astype(bf16))


def map_back(map_ref, mapg_ref, heads, hdim):
    one, zero = jnp.ones((hdim, map_ref.shape[2]), bf16), jnp.zeros((hdim, map_ref.shape[2]), bf16)
    for p in range(heads // 2):
        left = jnp.concatenate([map_ref[2 * p], zero, one, zero], axis=0)
        right = jnp.concatenate([zero, map_ref[2 * p + 1], zero, one], axis=0)
        mapg_ref[p] = jnp.concatenate([left, right], axis=1)


def rows_grad(logs, mapg, rows_bf, factor):
    r = mm_nt(jnp.concatenate(logs, axis=1), mapg)
    return (factor * r[:, :128] - (factor * factor) * rows_bf.astype(f32) * r[:, 128:]).astype(bf16)


def weight_parts(step, steps, lhs_ref, pg_ref, keep_ref, send_ref, width):
    own = width // 2
    for xr in range(2):

        @pl.when(step == steps + xr)
        def _():
            rhs = [pg_ref[:, pl.ds(c * width + half_cols(xr, own), own)] for c in range(pg_ref.shape[1] // width)]
            put_grad(keep_ref, send_ref, mm(lhs_ref[...], jnp.concatenate(rhs, axis=1)))


def key_back(
    len_ref, kv_ref, tok_ref, map_ref, own_ref, tot_ref, span_ref, recv_ref,
    *refs,
    half, nseg, heads, hdim, steps, dp_count, sort
):
    pgo_ref, vec_ref, keep_ref, send_ref, sg_ref, sgt_ref, mapg_ref, pg_ref, lhs_ref, tmp_ref = refs[-10:]
    step = pl.program_id(0)
    rows, width = tok_ref.shape
    feat = map_ref.shape[2]
    wide = nseg * hdim
    starts, ends = bounds(len_ref, nseg)
    here = spanning(ends, half)
    first = lax.axis_index("x") * half + step * rows
    factor = hdim ** (-0.25)

    @pl.when(step == 0)
    def _():
        vec_ref[...] = jnp.zeros_like(vec_ref)
        put_states(own_ref, tot_ref, span_ref, recv_ref, sg_ref, sgt_ref, here, nseg, heads, hdim)
        map_back(map_ref, mapg_ref, heads, hdim)

    @pl.when(step < steps)
    def _():
        at = pl.multiple_of(step * rows, 128)
        mine = pl.ds(at, rows)
        seg_wide, seg8 = seg_masks(first, rows, hdim, nseg, starts, ends)
        seg_wide_bf, seg8_bf = as_bf(seg_wide), as_bf(seg8)
        low_half = iota((rows, 128), 1) < hdim
        for p in range(heads // 2):
            k_cols, v_cols = slice(128 * p, 128 * (p + 1)), slice(width + 128 * p, width + 128 * (p + 1))
            k_pair = kv_ref[:, k_cols]
            v_reps = replicate(kv_ref[:, v_cols], low_half, hdim)
            logs, folded = [], []
            for j in range(2):
                h = 2 * p + j
                logits = factor * mm(k_pair, head_map(map_ref, h)) - (0.5 * factor * factor) * key_offset(k_pair, low_half, j)
                feats = jnp.exp(logits)
                lhs = jnp.concatenate([v_reps[j]] * 2, axis=1) * seg_wide_bf
                state_grad = sg_ref[wide * h : wide * (h + 1), :]
                slope = mm(lhs, state_grad) + mm(seg8_bf, sgt_ref[:, feat * h : feat * (h + 1)])
                logs.append((slope * feats).astype(bf16))
                r = jnp.where(seg_wide, mm_nt(feats.astype(bf16), state_grad), 0.0)
                folded.append(r[:, :128] + r[:, 128:])
            pg_ref[mine, k_cols] = rows_grad(logs, mapg_ref[p], k_pair, factor)
            pg_ref[mine, v_cols] = fold_pair(folded, low_half, hdim).astype(bf16)
        grads = pg_ref[mine, :]
        pgo_ref[...] = grads
        add_row(vec_ref, 1, grads[:, :width].astype(f32))
        add_row(vec_ref, 2, grads[:, width:].astype(f32))
        put_transposed(lhs_ref, tmp_ref, tok_ref[...], at, row_sources(dp_count) if sort else [])

    weight_parts(step, steps, lhs_ref, pg_ref, keep_ref, send_ref, width)


def query_back(
    len_ref, q_ref, num_ref, dgm_ref, tok_ref, map_ref, own_ref, tot_ref, span_ref, recv_ref,
    *refs,
    half, nseg, heads, hdim, steps, dp_count, sort
):
    pgo_ref, vec_ref, keep_ref, send_ref, st_ref, totp_ref, mapg_ref, pg_ref, lhs_ref, tmp_ref = refs[-10:]
    step = pl.program_id(0)
    rows, width = tok_ref.shape
    feat = map_ref.shape[2]
    wide = nseg * hdim
    starts, ends = bounds(len_ref, nseg)
    first = lax.axis_index("x") * half + step * rows
    factor = hdim ** (-0.25)

    @pl.when(step == 0)
    def _():
        vec_ref[...] = jnp.zeros_like(vec_ref)
        put_states(own_ref, tot_ref, span_ref, recv_ref, st_ref, totp_ref, spanning(ends, half), nseg, heads, hdim)
        map_back(map_ref, mapg_ref, heads, hdim)

    @pl.when(step < steps)
    def _():
        at = pl.multiple_of(step * rows, 128)
        mine = pl.ds(at, rows)
        seg_wide, _ = seg_masks(first, rows, hdim, nseg, starts, ends)
        seg_wide_bf = as_bf(seg_wide)
        low_half = iota((rows, 128), 1) < hdim
        den_m = dgm_ref[...]
        for p in range(heads // 2):
            cols = slice(128 * p, 128 * (p + 1))
            q_pair = q_ref[:, cols]
            reps = replicate(num_ref[:, cols], low_half, hdim)
            logs = []
            for j in range(2):
                h = 2 * p + j
                proj = mm(q_pair, head_map(map_ref, h))
                shifted = proj - jnp.max(proj, axis=-1, keepdims=True)
                lhs = jnp.concatenate([reps[j]] * 2, axis=1) * seg_wide_bf
                slope = mm(lhs, st_ref[wide * h : wide * (h + 1), :]) + mm(den_m, totp_ref[:, feat * h : feat * (h + 1)])
                slope = slope * jnp.exp(factor * shifted)
                peak = jnp.where(shifted == 0.0, 1.0, 0.0)
                share = jnp.sum(slope, axis=-1, keepdims=True) / jnp.sum(peak, axis=-1, keepdims=True)
                logs.append((slope - peak * share).astype(bf16))
            pg_ref[mine, cols] = rows_grad(logs, mapg_ref[p], q_pair, factor)
        grads = pg_ref[mine, :]
        pgo_ref[...] = grads
        add_row(vec_ref, 0, grads.astype(f32))
        put_transposed(lhs_ref, tmp_ref, tok_ref[...], at, row_sources(dp_count) if sort else [])

    weight_parts(step, steps, lhs_ref, pg_ref, keep_ref, send_ref, width)


def token_grads(agrad_ref, pgq_ref, pgkv_ref, wq_ref, wk_ref, wv_ref, *refs):
    out_ref = refs[-1]
    width = agrad_ref.shape[1]
    total = agrad_ref[...].astype(f32) + mm_nt(pgq_ref[...], wq_ref[...])
    total += mm_nt(pgkv_ref[:, :width], wk_ref[...])
    out_ref[...] = (total + mm_nt(pgkv_ref[:, width:], wv_ref[...])).astype(bf16)


def params(micros):
    return dict(
        compiler_params=pltpu.CompilerParams(vmem_limit_bytes=vmem_limit),
        cost_estimate=pl.CostEstimate(flops=int(micros * 1.1e9), bytes_accessed=int(micros * 1e6), transcendentals=0),
    )


def whole(shape):
    return pl.BlockSpec(shape, lambda i: (0,) * len(shape), pipeline_mode=pl.Buffered(1))


def resident(shape):
    return pl.BlockSpec(shape, lambda i: (0,) * len(shape))


def sds(shape, dtype):
    return jax.ShapeDtypeStruct(shape, dtype)


every_axis = ("z", "y", "c", "x")


def exchange(values, mask, dp_count):
    return lax.ppermute(values, every_axis, [(i, i ^ mask) for i in range(2 * dp_count)])


def sort_rows(keep, send, dp_count):
    _, _, blocks, quarter, _ = keep.shape
    natural = jnp.stack([keep, send]).transpose(0, 1, 4, 2, 3, 5).reshape(dp_count, -1, 2, blocks, 128)
    rows = jnp.take(natural, jnp.stack(row_sources(dp_count)), axis=0)
    rows = rows.reshape(2, 2, quarter, 2, blocks, 128).transpose(0, 1, 3, 4, 2, 5)
    return rows[0], rows[1]


def route(name, arrays, outs, moves, vec=None, after=()):
    rows = arrays[0].shape[-2]
    grid = 2 if rows % 32 == 0 else 1
    own, got, send = vec if vec is not None else (None, None, None)
    extra = [own] if vec is not None else []
    if vec is not None:
        count, blocks = own.shape[0], own.shape[1] // 128
        assert grid == 2 and 2 * count * blocks == rows

    def spec(shape):
        lead = len(shape) - 2
        return pl.BlockSpec(tuple(shape[:lead]) + (rows // grid, 128), lambda i: (0,) * lead + (i, 0))

    def kernel(*refs):
        ins, results = refs[: len(arrays)], refs[len(arrays) + len(extra) + len(after) :]
        for out, to, parts in moves:
            total = ins[parts[0][0]][parts[0][1]].astype(f32)
            for n, at in parts[1:]:
                total = total + ins[n][at].astype(f32)
            results[out][to] = total.astype(bf16)
        if vec is not None:
            step = pl.program_id(0)
            sums_ref = results[-1]

            @pl.when(step == 0)
            def _():
                sums_ref[...] = refs[len(arrays)][...]

            if got is not None:
                other = ins[got[0]][got[1]].astype(f32)
                sums_ref[...] += jnp.concatenate([other[b * count : (b + 1) * count] for b in range(blocks)], axis=1)
            if send is not None:
                sums = sums_ref[...]
                hi = sums.astype(bf16)
                part = jnp.where(step == 0, hi.astype(f32), sums - hi.astype(f32)).astype(bf16)
                rows_of = [part[:, 128 * b : 128 * (b + 1)] for b in range(blocks)]
                results[send[0]][send[1]] = jnp.concatenate(rows_of, axis=0)

    shapes = [sds(v, bf16) for v in outs]
    specs = [spec(v) for v in outs]
    if vec is not None:
        shapes.append(sds(own.shape, f32))
        specs.append(resident(own.shape))
    return pl.pallas_call(
        kernel,
        name=name,
        grid=(grid,),
        in_specs=[spec(a.shape) for a in arrays] + [resident(v.shape) for v in extra] + [pl.BlockSpec(memory_space=pl.ANY)] * len(after),
        out_specs=specs,
        out_shape=shapes,
        **params(3),
    )(*arrays, *extra, *after)


def first_moves(groups, left):
    moves, n = [], 0
    for array, blocks in groups:
        for b in range(blocks):
            for y in range(2):
                for x in range(2):
                    parts = [(array, (y, x, b)), (array + 1, (y, x, b))]
                    moves.append((x, (y, n), parts) if n < left else (2 + y, (x, n - left), parts))
            n += 1
    return moves


def second_moves(array, left, right, out):
    moves = []
    for b in range(left):
        moves += [(out if y == 0 else out + 1, (b,), [(array, (y, b)), (array + 1, (y, b))]) for y in range(2)]
    for b in range(right):
        moves += [(out if x == 0 else out + 2, (left + b if x == 0 else b,), [(array + 2, (x, b)), (array + 3, (x, b))]) for x in range(2)]
    return moves


def third_sum(keep, left_got, right_got):
    return added(bf16, keep, jnp.concatenate([left_got, right_got], axis=0))


def added(dtype, *parts):
    return functools.reduce(jnp.add, [p.astype(f32) for p in parts]).astype(dtype)


def odd_even(part, count):
    pairs = part.reshape(part.shape[0], count // 2, 2, -1, 128)
    return [pairs[:, :, k].reshape(part.shape[0], -1, 128) for k in range(2)]


def columns(part):
    return part.transpose(1, 0, 2).reshape(part.shape[1], -1)


def body(
    tokens, lengths, feature_map, qkv_weight, qkv_bias, out_weight, out_bias, ln1_gain, ln1_shift,
    up_weight, up_bias, down_weight, down_bias, ln2_gain, ln2_shift, cotangent,
):
    half, width = tokens.shape
    heads, hdim, feat = feature_map.shape
    nseg = lengths.shape[1]
    hidden_units = up_weight.shape[1]
    wide = nseg * hdim
    dp_count = lax.axis_size(("z", "y", "c"))
    assert lax.axis_size("x") == 2 and dp_count & (dp_count - 1) == 0 and dp_count >= 8
    assert 2 * hdim == 128 and wide == 256 and 8 * heads <= 128
    sort = (width // dp_count) % 16 == 0
    layout = dict(dp_count=dp_count, sort=sort)
    wq, wk, wv = (qkv_weight[:, c, :] for c in range(3))
    rows = min(256, half)
    steps = half // rows
    big = min(512, half)
    span_rows = heads * hdim + 16
    state_shapes = [
        sds((heads * wide, feat), bf16), sds((heads * 8, feat), f32),
        sds((span_rows - 16, feat), f32), sds((span_rows, feat), bf16),
    ]
    state_specs = [resident(s.shape) for s in state_shapes]
    lens = pl.BlockSpec(memory_space=pltpu.SMEM)
    acc = pltpu.VMEM((heads, wide + 16, feat), f32)
    features = whole(feature_map.shape)
    square = whole((width, width))

    def tile(cols):
        return pl.BlockSpec((rows, cols), lambda i: (jnp.minimum(i, steps - 1), 0))

    def vector(size):
        return pl.BlockSpec((size,), lambda i: (0,))

    static = dict(half=half, nseg=nseg, heads=heads, hdim=hdim)
    dense = 2 * half * width

    def parts(cols, before, count):
        shape = sds((2, 2, cols // 128, width // 4, 128), bf16)
        at = lambda i: (0, jnp.maximum(i - before, 0) // count, 0, 0, 0)
        return [pl.BlockSpec((2, 1, cols // 128, width // 4, 128), at)] * 2, [shape] * 2

    def run(kernel, name, grid, in_specs, args, after, **more):
        fence = [pl.BlockSpec(memory_space=pl.ANY)] * len(after)
        return pl.pallas_call(kernel, name=name, grid=grid, in_specs=list(in_specs) + fence, **more)(*args, *after)

    def over_core(keep, send):
        if not sort:
            keep, send = sort_rows(keep, send, dp_count)
        return keep, exchange(send, 2, dp_count)

    kv, own, tot, span, send = pl.pallas_call(
        functools.partial(forward_keys, **static),
        name="key_states",
        grid=(steps,),
        in_specs=[lens, tile(width), square, square, whole((3, width)), features],
        out_specs=[tile(2 * width)] + state_specs,
        out_shape=[sds((half, 2 * width), bf16)] + state_shapes,
        scratch_shapes=[acc],
        **params(12),
    )(lengths, tokens, wk, wv, qkv_bias, feature_map)
    recv = exchange(send, 1, dp_count)
    q_rows, q_feats = pl.pallas_call(
        functools.partial(forward_queries, heads=heads, hdim=hdim),
        name="query_features",
        grid=(steps,),
        in_specs=[tile(width), square, whole((3, width)), features],
        out_specs=[tile(width), tile(heads * feat)],
        out_shape=[sds((half, width), bf16), sds((half, heads * feat), bf16)],
        **params(7),
    )(tokens, wq, qkv_bias, feature_map)

    chunk = 512
    count = hidden_units // chunk
    half_w, half_u = width // 2, hidden_units // 2
    vec_rows = 6 + hidden_units // width
    vec_rows += -vec_rows % 8

    def tiles(cols, size, before):
        per = cols // size

        def at(i):
            t = jnp.clip(i - before, 0, 2 * per - 1)
            return (0, t // per, t % per, 0, 0)

        shape = sds((2, 2, cols // 128, width // 4, 128), bf16)
        return [pl.BlockSpec((2, 1, size // 128, width // 4, 128), at)] * 2, [shape] * 2

    d_specs, d_shapes = tiles(half_u, chunk, steps)
    u_specs, u_shapes = tiles(half_u, chunk, steps + count)
    o_specs, o_shapes = tiles(half_w, half_w, steps + 2 * count)
    hbm = pl.BlockSpec(memory_space=pl.ANY)
    (output, agrad, num_grad, den_m, vec_1, s_own, s_tot, s_span, s_send, d_keep, d_send, u_keep, u_send, o_keep, o_send) = run(
        functools.partial(chain, chunk=chunk, steps=steps, **layout, **static),
        "chain",
        (steps + 2 * count + 2,),
        [lens, tile(width), tile(heads * feat), tile(width)]
        + [whole(v.shape) for v in (own, tot, span, recv)]
        + [square, vector(width), vector(width), vector(width)]
        + [hbm, vector(hidden_units), hbm]
        + [vector(width)] * 3,
        (
            lengths, tokens, q_feats, cotangent, own, tot, span, recv, out_weight, out_bias, ln1_gain, ln1_shift,
            up_weight, up_bias, down_weight, down_bias, ln2_gain, ln2_shift,
        ),
        (),
        out_specs=[tile(c) for c in (width, width, width, 128)] + [resident((vec_rows, width))] + state_specs + d_specs + u_specs + o_specs,
        out_shape=[sds((half, c), bf16) for c in (width, width, width, 128)]
        + [sds((vec_rows, width), f32)]
        + state_shapes + d_shapes + u_shapes + o_shapes,
        scratch_shapes=[
            pltpu.VMEM((heads * wide, feat), bf16),
            pltpu.VMEM((128, heads * feat), bf16),
            acc,
            pltpu.VMEM((half, hidden_units), bf16),
            pltpu.VMEM((half, hidden_units), bf16),
            pltpu.VMEM((half, width), bf16),
            pltpu.VMEM((rows, hidden_units), bf16),
            pltpu.VMEM((width, half), bf16),
            pltpu.VMEM((width, half), bf16),
            pltpu.VMEM((width, half), bf16),
            pltpu.VMEM((width, rows), bf16),
            pltpu.VMEM(up_weight.shape, bf16),
            pltpu.VMEM(down_weight.shape, bf16),
            pltpu.SemaphoreType.DMA((2,)),
        ],
        **params(66),
    )
    s_recv = exchange(s_send, 1, dp_count)
    d_keep, d_got = over_core(d_keep, d_send)
    u_keep, u_got = over_core(u_keep, u_send)
    o_keep, o_got = over_core(o_keep, o_send)
    block = (width // 4, 128)
    d_n, u_n, o_n = half_u // 128, half_u // 128, half_w // 128
    d_l, uo_l, qkv_n, qkv_l = d_n // 2, (u_n + o_n) // 2, 3 * o_n, 3 * o_n // 2
    d_r, uo_r, qkv_r = d_n - d_l, u_n + o_n - uo_l, qkv_n - qkv_l
    pair = lambda n: (2, n) + block
    d_lk, d_ls, d_rk, d_rs = route("down_1", [d_keep, d_got], [pair(d_l)] * 2 + [pair(d_r)] * 2, first_moves([(0, d_n)], d_l))
    x_got, y_got = exchange(d_ls, 1, dp_count), exchange(d_rs, 4, dp_count)
    rows = min(512, half)
    steps = half // rows

    def back_scratch(n):
        return [
            pltpu.VMEM((heads // 2, 4 * hdim, 2 * feat), bf16),
            pltpu.VMEM((half, n * width), bf16),
            pltpu.VMEM((width, half), bf16),
            pltpu.VMEM((width, rows), bf16),
        ]

    q_specs, q_shapes = parts(half_w, steps, 1)
    state_scratch = [pltpu.VMEM((heads * wide, feat), bf16), pltpu.VMEM((128, heads * feat), bf16)]
    pg_q, vec_2, q_keep, q_send = run(
        functools.partial(query_back, steps=steps, **layout, **static),
        "query_back",
        (steps + 2,),
        [lens, tile(width), tile(width), tile(128), tile(width), features] + [whole(v.shape) for v in (own, tot, span, recv)],
        (lengths, q_rows, num_grad, den_m, tokens, feature_map, own, tot, span, recv),
        (d_lk,),
        out_specs=[tile(width), resident((8, width))] + q_specs,
        out_shape=[sds((half, width), bf16), sds((8, width), f32)] + q_shapes,
        scratch_shapes=state_scratch + back_scratch(1),
        **params(18),
    )
    q_keep, q_got = over_core(q_keep, q_send)
    arrays = [d_lk, x_got, d_rk, y_got, u_keep, u_got, o_keep, o_got]
    moves = second_moves(0, d_l, d_r, 0)
    shift = {1: 4, 2: 3}
    moves = [(shift.get(out, out), at, terms) for out, at, terms in moves]
    for out, at, terms in first_moves([(4, u_n), (6, o_n)], uo_l):
        place = at[0] * (uo_l if out < 2 else uo_r) + at[1]
        if out in (0, 2):
            moves.append((1 if out == 0 else 2, at, terms))
        else:
            moves.append((3, (d_r + place,), terms) if out == 1 else (4, (d_l + place,), terms))
    flat = lambda n: (n,) + block
    d_part, uo_lk, uo_rk, x_send, y_send = route(
        "down_2_up_1", arrays, [flat(d_n), pair(uo_l), pair(uo_r), flat(d_r + 2 * uo_l), flat(d_l + 2 * uo_r)], moves
    )
    x_got, y_got = exchange(x_send, 1, dp_count), exchange(y_send, 4, dp_count)

    kv_specs, kv_shapes = parts(2 * half_w, steps, 1)
    pg_kv, vec_3, kv_keep, kv_send = run(
        functools.partial(key_back, steps=steps, **layout, **static),
        "key_back",
        (steps + 2,),
        [lens, tile(2 * width), tile(width), features] + [whole(v.shape) for v in (s_own, s_tot, s_span, s_recv)],
        (lengths, kv, tokens, feature_map, s_own, s_tot, s_span, s_recv),
        (d_part, vec_2),
        out_specs=[tile(2 * width), resident((8, width))] + kv_specs,
        out_shape=[sds((half, 2 * width), bf16), sds((8, width), f32)] + kv_shapes,
        scratch_shapes=state_scratch + back_scratch(2),
        **params(18),
    )
    kv_keep, kv_got = over_core(kv_keep, kv_send)
    up_rows = hidden_units // width
    vec = jnp.concatenate([vec_1[: 6 + up_rows], (vec_2 + vec_3)[:3]], axis=0)
    vec = jnp.pad(vec, ((0, -vec.shape[0] % 16), (0, 0)))
    vec_got = exchange(vec, 2, dp_count)
    d_x, uo_x = x_got[:d_r], x_got[d_r:].reshape(pair(uo_l))
    d_y, uo_y = y_got[:d_l], y_got[d_l:].reshape(pair(uo_r))
    uo_part, uo_ls, uo_rs = route(
        "up_2", [uo_lk, uo_x, uo_rk, uo_y], [flat(uo_l + uo_r), flat(uo_l), flat(uo_r)], second_moves(0, uo_l, uo_r, 0)
    )
    x_got, y_got = exchange(uo_rs, 1, dp_count), exchange(uo_ls, 4, dp_count)
    z_bits = [8 << b for b in range((dp_count // 4).bit_length() - 1)]
    left_z = [dp_count // 4 >> n for n in range(len(z_bits))]

    def start_z(part, n):
        keep, send = odd_even(part, left_z[n])
        return keep, exchange(send, z_bits[n], dp_count)

    def end_z(keep, got, n):
        return added(bf16 if n + 1 < len(z_bits) else f32, keep, got)

    down_z = start_z(third_sum(d_part, d_y, d_x), 0)
    qkv_lk, qkv_ls, qkv_rk, qkv_rs, vec = route(
        "qkv_1",
        [q_keep, q_got, kv_keep, kv_got],
        [pair(qkv_l), flat(2 * qkv_l + 1), pair(qkv_r), pair(qkv_r)],
        [
            (out, (at[0] * qkv_l + at[1],) if out == 1 else at, terms)
            for out, at, terms in first_moves([(0, o_n), (2, 2 * o_n)], qkv_l)
        ],
        (vec + vec_got, None, (1, (2 * qkv_l,))),
        (uo_part, down_z[0]),
    )
    qkv_x, qkv_y = exchange(qkv_ls, 1, dp_count), exchange(qkv_rs, 4, dp_count)

    grad_tokens = run(
        token_grads,
        "token_grads",
        (steps,),
        [tile(width), tile(width), tile(2 * width), square, square, square],
        (agrad, pg_q, pg_kv, wq, wk, wv),
        (qkv_lk,),
        out_specs=tile(width),
        out_shape=sds((half, width), bf16),
        **params(8),
    )
    up_z = start_z(third_sum(uo_part, y_got, x_got), 0)
    down_part = end_z(*down_z, 0)
    if len(z_bits) > 1:
        down_z = start_z(down_part, 1)
    moves = []
    for out, at, terms in second_moves(0, qkv_l, qkv_r, 0):
        terms = [(n, (at_n[0] * qkv_l + at_n[1],) if n == 1 else at_n) for n, at_n in terms]
        moves.append((out, at, terms))
    qkv_part, qkv_ls, qkv_rs, vec = route(
        "qkv_2",
        [qkv_lk, qkv_x, qkv_rk, qkv_y],
        [flat(qkv_n), flat(qkv_l + 1), flat(qkv_r)],
        moves,
        (vec, (1, (2 * qkv_l,)), (1, (qkv_l,))),
        (up_z[0], down_z[0], grad_tokens),
    )
    qkv_x, qkv_y = exchange(qkv_rs, 1, dp_count), exchange(qkv_ls, 4, dp_count)

    def rest(part, z, first):
        for n in range(first, len(z_bits)):
            part = end_z(*z, n)
            if n + 1 < len(z_bits):
                z = start_z(part, n + 1)
        return columns(part)

    d_down = rest(down_part, down_z, 1) if len(z_bits) > 1 else columns(down_part)
    d_up_out = rest(None, up_z, 0)

    def add_vec(vec, got):
        count, blocks = vec.shape[0], vec.shape[1] // 128
        got = got.reshape(-1, 128).astype(f32)
        got = got[: count * blocks] + got[count * blocks :]
        return vec + jnp.concatenate([got[b * count : (b + 1) * count] for b in range(blocks)], axis=1)

    def vec_rows_of(vec):
        hi = vec.astype(bf16)
        lo = (vec - hi.astype(f32)).astype(bf16)
        return jnp.concatenate([v[:, 128 * b : 128 * (b + 1)] for v in (hi, lo) for b in range(vec.shape[1] // 128)], axis=0)

    vec = add_vec(vec, qkv_y[qkv_l])
    part = third_sum(qkv_part, qkv_y[:qkv_l], qkv_x)
    for n, bit in enumerate(z_bits):
        keep, send = odd_even(part, left_z[n])
        got = exchange(jnp.concatenate([send.reshape(-1, 128), vec_rows_of(vec)], axis=0), bit, dp_count)
        size = send.size // 128
        vec = add_vec(vec, got[size:])
        part = end_z(keep, got[:size].reshape(send.shape), n)
    d_qkv = part.reshape(3, o_n, -1, 128).transpose(2, 0, 1, 3).reshape(-1, 3, half_w)
    return (
        output,
        grad_tokens,
        d_qkv,
        vec[6 + up_rows : 9 + up_rows],
        d_up_out[:, half_u:],
        vec[3],
        vec[4],
        vec[5],
        d_up_out[:, :half_u],
        vec[6 : 6 + up_rows].reshape(-1),
        d_down,
        vec[0],
        vec[1],
        vec[2],
    )


def solution(mesh):
    dp_count = mesh.shape["dp"]
    fine = jax.sharding.Mesh(mesh.devices.reshape(dp_count // 4, 2, 2, 2), every_axis)
    dp = ("z", "y", "c")
    rows = P(every_axis, None)
    in_specs = (rows, P(dp, None)) + (P(),) * 13 + (rows,)
    out_specs = (
        rows, rows, P(dp, None, "x"), P(), P(dp, "x"), P(), P(), P(),
        P(dp, "x"), P(), P(dp, "x"), P(), P(), P(),
    )
    return jax.shard_map(body, mesh=fine, in_specs=in_specs, out_specs=out_specs, check_vma=False)
```

```python
import functools

import jax
import jax.numpy as jnp
from jax import lax
from jax.experimental import pallas as pl
from jax.experimental.pallas import tpu as pltpu
from jax.sharding import PartitionSpec as P

bf16 = jnp.bfloat16
f32 = jnp.float32
norm_epsilon = 1e-06
root_half = 0.7071067811865476
inv_root_tau = 0.3989422804014327
vmem_limit = 62 * 1024 * 1024
stream_lead = 6
nt_dims = (((1,), (1,)), ((), ()))


def mm(a, b):
    return jnp.dot(a, b, preferred_element_type=f32)


def mm_nt(a, b):
    return lax.dot_general(a, b, nt_dims, preferred_element_type=f32)


def iota(shape, dim):
    return lax.broadcasted_iota(jnp.int32, shape, dim)


def bounds(len_ref, nseg):
    starts, ends, run = [], [], jnp.int32(0)
    for s in range(nseg):
        starts.append(run)
        run = run + len_ref[0, s]
        ends.append(run)
    return starts, ends


def spanning(ends, half):
    count = jnp.int32(0)
    for end in ends:
        count = count + (end < half).astype(jnp.int32)
    return count


def pick(index, values):
    out = jnp.full(index.shape, values[-1], jnp.int32)
    for s in range(len(values) - 2, -1, -1):
        out = jnp.where(index == s, values[s], out)
    return out


def inside(pos, index, starts, ends):
    return jnp.logical_and(pos >= pick(index, starts), pos < pick(index, ends))


def as_bf(mask):
    return jnp.where(mask, 1.0, 0.0).astype(bf16)


def split_hi_lo(v):
    hi = v.astype(bf16)
    lo = (v - hi.astype(f32)).astype(bf16)
    return jnp.concatenate([hi, lo], axis=1)


def masked_rows(rows_t, lane_masks, tail):
    return jnp.concatenate([rows_t * m for m in lane_masks] + [tail], axis=0)


def head_map(map_ref, h):
    m = map_ref[h]
    z = jnp.zeros_like(m)
    return jnp.concatenate([m, z] if h % 2 == 0 else [z, m], axis=0)


def key_offset(k_pair, low_half, j):
    sq = jnp.square(k_pair.astype(f32))
    mine = low_half if j == 0 else jnp.logical_not(low_half)
    return jnp.sum(jnp.where(mine, sq, 0.0), axis=-1, keepdims=True)


def put_states(own_ref, tot_ref, span_ref, recv_ref, st_ref, totp_ref, here, nseg, heads, hdim):
    wide = nseg * hdim
    feat = st_ref.shape[1]
    recv_tot = recv_ref[heads * hdim :, :].astype(f32)
    seg_row = iota((8, feat), 0)
    for h in range(heads):
        if own_ref is not None:
            st_ref[h * wide : (h + 1) * wide, :] = own_ref[h * wide : (h + 1) * wide, :]
        both = span_ref[h * hdim : (h + 1) * hdim, :] + recv_ref[h * hdim : (h + 1) * hdim, :].astype(f32)
        at = pl.multiple_of(h * wide + here * hdim, hdim)
        st_ref[pl.ds(at, hdim), :] = both.astype(bf16)
        tot = tot_ref[8 * h : 8 * h + 8, :]
        tot = jnp.where(seg_row == here, tot + recv_tot[h : h + 1, :], tot)
        parts = [tot]
        if h > 0:
            parts.insert(0, jnp.zeros((8 * h, feat), f32))
        if 8 * h + 8 < 128:
            parts.append(jnp.zeros((128 - 8 * h - 8, feat), f32))
        totp_ref[:, feat * h : feat * (h + 1)] = jnp.concatenate(parts, axis=0).astype(bf16)


def emit_states(acc_ref, own_ref, tot_ref, span_ref, send_ref, here, nseg, heads, hdim):
    wide = nseg * hdim
    feat = acc_ref.shape[2]
    for h in range(heads):
        own_ref[h * wide : (h + 1) * wide, :] = acc_ref[h, 0:wide, :].astype(bf16)
        tot_ref[8 * h : 8 * h + 8, :] = acc_ref[h, wide : wide + 8, :]
        at = pl.multiple_of(here * hdim, hdim)
        part = acc_ref[h, pl.ds(at, hdim), :]
        span_ref[h * hdim : (h + 1) * hdim, :] = part
        send_ref[h * hdim : (h + 1) * hdim, :] = part.astype(bf16)
    row = iota((16, feat), 0)
    seg_row = iota((8, feat), 0)
    tots = jnp.zeros((16, feat), f32)
    for h in range(heads):
        mine = jnp.sum(jnp.where(seg_row == here, acc_ref[h, wide : wide + 8, :], 0.0), axis=0, keepdims=True)
        tots = jnp.where(row == h, mine, tots)
    send_ref[heads * hdim :, :] = tots.astype(bf16)


def lane_segment_masks(first, rows, hdim, starts, ends):
    pos = first + iota((hdim, rows), 1)
    masks = [as_bf(jnp.logical_and(pos >= a, pos < b)) for a, b in zip(starts, ends)]
    pos = first + iota((16, rows), 1)
    seg = iota((16, rows), 0)
    tail = as_bf(jnp.logical_and(seg < len(starts), inside(pos, seg, starts, ends)))
    return masks, tail


def seg_masks(first, rows, hdim, nseg, starts, ends):
    pos = first + iota((rows, nseg * hdim), 0)
    wide = inside(pos, iota((rows, nseg * hdim), 1) >> (hdim.bit_length() - 1), starts, ends)
    lane8 = iota((rows, 128), 1) & 7
    pos = first + iota((rows, 128), 0)
    eight = jnp.logical_and(lane8 < nseg, inside(pos, lane8, starts, ends))
    return wide, eight


def block_of(p, dp_count):
    top = dp_count.bit_length() - 1
    return (p >> (top - 1)) & 1 | ((p >> (top - 2)) & 1) << 1 | (p & (dp_count // 4 - 1)) << 2


def dp_index():
    return (lax.axis_index("z") * 2 + lax.axis_index("y")) * 2 + lax.axis_index("c")


def row_sources(dp_count):
    return [jnp.bitwise_xor(dp_index(), block_of(p, dp_count)) for p in range(dp_count)]


def put_transposed(lhs_ref, tmp_ref, values, at, sources):
    rows, width = values.shape
    cols = pl.ds(at, rows)
    if not sources:
        lhs_ref[:, cols] = values.T
        return
    block = width // len(sources)
    tmp_ref[...] = values.T
    for p, source in enumerate(sources):
        lhs_ref[p * block : (p + 1) * block, cols] = tmp_ref[pl.ds(pl.multiple_of(source * block, 16), block), :]


def fold_pair(folded, low_half, hdim):
    straight = jnp.where(low_half, folded[0], folded[1])
    crossed = jnp.where(low_half, folded[1], folded[0])
    return straight + pltpu.roll(crossed, hdim, 1)


def forward_keys(
    len_ref, tok_ref, wk_ref, wv_ref, b_ref, map_ref, kv_ref, own_ref, tot_ref, span_ref, send_ref, acc_ref,
    *, half, nseg, heads, hdim
):
    step = pl.program_id(0)
    rows, width = tok_ref.shape
    starts, ends = bounds(len_ref, nseg)
    here = spanning(ends, half)
    first = lax.axis_index("x") * half + step * rows
    factor = hdim ** (-0.25)

    @pl.when(step == 0)
    def _():
        acc_ref[...] = jnp.zeros_like(acc_ref)

    masks, tail = lane_segment_masks(first, rows, hdim, starts, ends)
    tok = tok_ref[...]
    keys = (mm(tok, wk_ref[...]) + b_ref[1:2, :]).astype(bf16)
    vals = (mm(tok, wv_ref[...]) + b_ref[2:3, :]).astype(bf16)
    kv_ref[:, :width] = keys
    kv_ref[:, width:] = vals
    low_half = iota((rows, 128), 1) < hdim
    for p in range(heads // 2):
        k_pair = keys[:, 128 * p : 128 * (p + 1)]
        v_t = vals[:, 128 * p : 128 * (p + 1)].T
        for j in range(2):
            h = 2 * p + j
            logits = factor * mm(k_pair, head_map(map_ref, h)) - (0.5 * factor * factor) * key_offset(k_pair, low_half, j)
            feats = jnp.exp(logits).astype(bf16)
            lhs = masked_rows(v_t[j * hdim : (j + 1) * hdim, :], masks, tail)
            acc_ref[h] += mm(lhs, feats)

    @pl.when(step == pl.num_programs(0) - 1)
    def _():
        emit_states(acc_ref, own_ref, tot_ref, span_ref, send_ref, here, nseg, heads, hdim)


def forward_queries(tok_ref, wq_ref, b_ref, map_ref, q_ref, qf_ref, *, heads, hdim):
    feat = map_ref.shape[2]
    factor = hdim ** (-0.25)
    queries = (mm(tok_ref[...], wq_ref[...]) + b_ref[0:1, :]).astype(bf16)
    q_ref[...] = queries
    for h in range(heads):
        proj = mm(queries[:, 128 * (h // 2) : 128 * (h // 2 + 1)], head_map(map_ref, h))
        top = jnp.max(proj, axis=-1, keepdims=True)
        qf_ref[:, feat * h : feat * (h + 1)] = jnp.exp(factor * (proj - top)).astype(bf16)


def norm_backward(incoming, scaled, inverse, gain):
    weighted = incoming * gain
    return inverse * (
        weighted
        - jnp.mean(weighted, axis=-1, keepdims=True)
        - scaled * jnp.mean(weighted * scaled, axis=-1, keepdims=True)
    )


def norm_parts(values):
    centred = values - jnp.mean(values, axis=-1, keepdims=True)
    spread = jnp.mean(centred * centred, axis=-1, keepdims=True)
    inverse = lax.rsqrt(spread + norm_epsilon)
    return centred * inverse, inverse


def gelu_parts(u):
    cdf = 0.5 + 0.5 * lax.erf(u * root_half)
    return u * cdf, cdf + u * (inv_root_tau * jnp.exp(-0.5 * (u * u)))


def flat_row(ref):
    return ref[...].reshape(1, -1)


def add_row(vec_ref, row, values):
    vec_ref[row : row + 1, :] += jnp.sum(values, axis=0, keepdims=True)


def put_grad(keep_ref, send_ref, grad):
    quarter = grad.shape[0] // 4
    for b in range(grad.shape[1] // 128):
        cols = slice(128 * b, 128 * (b + 1))
        for y in range(2):
            keep_ref[y, 0, b] = grad[y * quarter : (y + 1) * quarter, cols].astype(bf16)
            send_ref[y, 0, b] = grad[(2 + y) * quarter : (3 + y) * quarter, cols].astype(bf16)


def half_cols(xr, half_width):
    x = lax.axis_index("x")
    return pl.multiple_of(jnp.bitwise_xor(x, xr) * half_width, 128)


def interleave(first, second, lead):
    alive = [first, second]
    turn = 0
    while alive:
        for stream in list(alive):
            if stream is second and turn < lead and first in alive:
                continue
            try:
                next(stream)
            except StopIteration:
                alive.remove(stream)
        turn += 1


def chain(
    len_ref, tok_ref, qf_ref, cot_ref, own_hbm, tot_ref, span_ref, recv_ref, wo_ref, bo_ref, g1_ref, s1_ref,
    wup_hbm, bup_ref, wdn_hbm, bdn_ref, g2_ref, s2_ref,
    out_ref, agrad_ref, num_ref, dgm_ref, normed_ref, mixed_ref, ugrad_hbm, vec_ref, sown_ref, stot_ref, sspan_ref, ssend_ref,
    dkeep_ref, dsend_ref,
    st_ref, totp_ref, expand_ref, gather_ref, acc_ref, act_ref, ugrad_ref, dlhs_ref, tmp_ref, wup_ref, wdn_ref, sem,
    *, half, nseg, heads, hdim, chunk, steps, dp_count, sort
):
    step = pl.program_id(0)
    rows, width = tok_ref.shape
    wide = nseg * hdim
    feat = st_ref.shape[1]
    hidden_units = wup_ref.shape[1]
    starts, ends = bounds(len_ref, nseg)
    here = spanning(ends, half)
    x = lax.axis_index("x")
    fetch = [pltpu.make_async_copy(wup_hbm, wup_ref, sem.at[0]), pltpu.make_async_copy(wdn_hbm, wdn_ref, sem.at[1])]
    fetch_own = pltpu.make_async_copy(own_hbm, st_ref, sem.at[2])

    def store(n, side):
        own = hidden_units // 2
        to = ugrad_hbm.at[pl.ds(pl.multiple_of(n * rows, 128), rows), pl.ds(half_cols(side, own), own)]
        return pltpu.make_async_copy(ugrad_ref.at[:, side * own : (side + 1) * own], to, sem.at[3 + side])

    @pl.when(step == 0)
    def _():
        fetch_own.start()
        fetch[0].start()
        fetch[1].start()
        fetch_own.wait()
        vec_ref[...] = jnp.zeros_like(vec_ref)
        acc_ref[...] = jnp.zeros_like(acc_ref)
        put_states(None, tot_ref, span_ref, recv_ref, st_ref, totp_ref, here, nseg, heads, hdim)
        shift = hdim.bit_length() - 1
        lane = iota((256, width), 0) & 127
        expand_ref[:, :width] = as_bf((lane >> 3) == (iota((256, width), 1) >> shift))
        expand_ref[:, width:] = as_bf(((iota((256, 128), 0) & 127) >> 3) == (iota((256, 128), 1) >> 3))
        for k in range(2):
            gather_ref[k * width : (k + 1) * width, :] = as_bf((iota((width, 128), 0) >> shift) == (iota((width, 128), 1) >> 3))
        fetch[0].wait()
        fetch[1].wait()

    def part(lo, size):
        mine = slice(lo, lo + size)
        at = pl.multiple_of(step * rows + lo, 128)
        first = x * half + step * rows + lo
        seg_wide, seg8 = seg_masks(first, size, hdim, nseg, starts, ends)
        low_half = iota((size, 128), 1) < hdim
        nums = []
        for p in range(heads // 2):
            folded = []
            for j in range(2):
                h = 2 * p + j
                r = mm_nt(qf_ref[mine, feat * h : feat * (h + 1)], st_ref[wide * h : wide * (h + 1), :])
                r = jnp.where(seg_wide, r, 0.0)
                folded.append(r[:, :128] + r[:, 128:])
            nums.append(fold_pair(folded, low_half, hdim))
            yield
        numer = jnp.concatenate(nums, axis=1)
        den_parts = split_hi_lo(jnp.where(seg8, mm_nt(qf_ref[mine, :], totp_ref[...]), 0.0))
        yield
        dead = jnp.where(first + iota((size, 128), 0) < ends[-1], 0.0, 1.0)
        spare = jnp.where(iota((size, 128), 1) < 8 * heads, dead, 1.0)
        den_w = mm(den_parts, expand_ref[...])
        inv_c = 1.0 / (den_w[:, width:] + spare)
        inv_w = 1.0 / (den_w[:, :width] + jnp.concatenate([dead] * (width // 128), axis=1))
        yield
        ratio = numer * inv_w
        mixed = ratio.astype(bf16)
        mixed_ref[mine, :] = mixed
        hidden = tok_ref[mine, :].astype(f32) + mm_nt(mixed, wo_ref[...]) + flat_row(bo_ref)
        yield
        scaled1, inverse1 = norm_parts(hidden)
        normed = scaled1 * flat_row(g1_ref) + flat_row(s1_ref)
        normed_bf = normed.astype(bf16)
        normed_ref[mine, :] = normed_bf
        yield

        count = hidden_units // chunk
        cols = [slice(c * chunk, (c + 1) * chunk) for c in range(count)]
        bup = flat_row(bup_ref)
        up = mm(normed_bf, wup_ref[:, cols[0]]) + bup[:, cols[0]]
        branch = normed + flat_row(bdn_ref)
        last = None
        for c in range(count):
            later = mm(normed_bf, wup_ref[:, cols[c + 1]]) + bup[:, cols[c + 1]] if c + 1 < count else None
            act, slope = gelu_parts(up)
            act = act.astype(bf16)
            act_ref[pl.ds(at, size), cols[c]] = act
            ugrad_ref[mine, cols[c]] = slope.astype(bf16)
            if last is not None:
                branch += mm_nt(last, wdn_ref[:, cols[c - 1]])
            last, up = act, later
            yield
        final = branch + mm_nt(last, wdn_ref[:, cols[count - 1]])
        yield
        scaled2, inverse2 = norm_parts(final)
        gain2 = flat_row(g2_ref)
        out_ref[mine, :] = (scaled2 * gain2 + flat_row(s2_ref)).astype(bf16)
        incoming = cot_ref[mine, :].astype(f32)
        grad_final = norm_backward(incoming, scaled2, inverse2, gain2)
        bgrad = grad_final.astype(bf16)
        add_row(vec_ref, 0, grad_final)
        add_row(vec_ref, 1, incoming * scaled2)
        add_row(vec_ref, 2, incoming)
        yield
        put_transposed(dlhs_ref, tmp_ref, bgrad, at, row_sources(dp_count) if sort else [])
        grad_normed = grad_final
        wide_grad = mm(bgrad, wdn_ref[:, cols[0]])
        last = None
        for c in range(count):
            later = mm(bgrad, wdn_ref[:, cols[c + 1]]) if c + 1 < count else None
            ugrad = (wide_grad * ugrad_ref[mine, cols[c]].astype(f32)).astype(bf16)
            ugrad_ref[mine, cols[c]] = ugrad
            sums = jnp.sum(ugrad.astype(f32), axis=0, keepdims=True)
            for k in range(0, chunk, 128):
                row, col = divmod(c * chunk + k, width)
                vec_ref[6 + row : 7 + row, col : col + 128] += sums[:, k : k + 128]
            if last is not None:
                grad_normed += mm_nt(last, wup_ref[:, cols[c - 1]])
            last, wide_grad = ugrad, later
            yield
        grad_normed += mm_nt(last, wup_ref[:, cols[count - 1]])
        yield

        grad_hidden = norm_backward(grad_normed, scaled1, inverse1, flat_row(g1_ref))
        add_row(vec_ref, 3, grad_hidden)
        add_row(vec_ref, 4, grad_normed * scaled1)
        add_row(vec_ref, 5, grad_normed)
        agrad = grad_hidden.astype(bf16)
        agrad_ref[mine, :] = agrad
        yield

        grad_mixed = mm(agrad, wo_ref[...])
        num_grad = (grad_mixed * inv_w).astype(bf16)
        num_ref[mine, :] = num_grad
        inner = split_hi_lo(grad_mixed * ratio)
        yield
        den_m = jnp.where(seg8, -(mm(inner, gather_ref[...]) * inv_c), 0.0).astype(bf16)
        dgm_ref[mine, :] = den_m
        den_t = den_m.T
        masks, _ = lane_segment_masks(first, size, hdim, starts, ends)
        pad = jnp.zeros((8, size), bf16)
        yield
        for p in range(heads // 2):
            num_t = num_grad[:, 128 * p : 128 * (p + 1)].T
            tails = den_t[16 * p : 16 * p + 16, :]
            for j in range(2):
                h = 2 * p + j
                tail = jnp.concatenate([tails[8 * j : 8 * j + 8, :], pad], axis=0)
                lhs = masked_rows(num_t[j * hdim : (j + 1) * hdim, :], masks, tail)
                acc_ref[h] += mm(lhs, qf_ref[mine, feat * h : feat * (h + 1)])
            yield

    @pl.when(jnp.logical_and(step >= 1, step <= steps))
    def _():
        store(step - 1, 0).wait()
        store(step - 1, 1).wait()

    @pl.when(step < steps)
    def _():
        size = rows // 2
        interleave(part(0, size), part(size, size), stream_lead)
        store(step, 0).start()
        store(step, 1).start()

    @pl.when(step == steps - 1)
    def _():
        emit_states(acc_ref, sown_ref, stot_ref, sspan_ref, ssend_ref, here, nseg, heads, hdim)

    own = hidden_units // 2
    count = hidden_units // chunk
    tile = step - steps

    @pl.when(tile >= 0)
    def _():
        xr = tile // (count // 2)
        at = half_cols(xr, own) + (tile - xr * (count // 2)) * chunk
        rhs = act_ref[:, pl.ds(pl.multiple_of(at, 128), chunk)]
        put_grad(dkeep_ref, dsend_ref, mm(dlhs_ref[...], rhs))


def up_out_grads(
    normed_ref, agrad_ref, mixed_ref, ugrad_ref,
    *refs,
    count, dp_count, sort
):
    ukeep_ref, usend_ref, okeep_ref, osend_ref, ulhs_ref, olhs_ref, tmp_ref = refs[-7:]
    step = pl.program_id(0)
    width = normed_ref.shape[1]

    @pl.when(step == 0)
    def _():
        put_transposed(ulhs_ref, tmp_ref, normed_ref[...], 0, row_sources(dp_count) if sort else [])

    @pl.when(step < count)
    def _():
        put_grad(ukeep_ref, usend_ref, mm(ulhs_ref[...], ugrad_ref[...]))

    @pl.when(step == count)
    def _():
        put_transposed(olhs_ref, tmp_ref, agrad_ref[...], 0, row_sources(dp_count) if sort else [])

    @pl.when(step >= count)
    def _():
        rhs = mixed_ref[:, pl.ds(half_cols(step - count, width // 2), width // 2)]
        put_grad(okeep_ref, osend_ref, mm(olhs_ref[...], rhs))


def replicate(pair, low_half, hdim):
    wide = pair.astype(f32)
    other = pltpu.roll(wide, hdim, 1)
    return (jnp.where(low_half, wide, other).astype(bf16), jnp.where(low_half, other, wide).astype(bf16))


def map_back(map_ref, mapg_ref, heads, hdim):
    one, zero = jnp.ones((hdim, map_ref.shape[2]), bf16), jnp.zeros((hdim, map_ref.shape[2]), bf16)
    for p in range(heads // 2):
        left = jnp.concatenate([map_ref[2 * p], zero, one, zero], axis=0)
        right = jnp.concatenate([zero, map_ref[2 * p + 1], zero, one], axis=0)
        mapg_ref[p] = jnp.concatenate([left, right], axis=1)


def rows_grad(logs, mapg, rows_bf, factor):
    r = mm_nt(jnp.concatenate(logs, axis=1), mapg)
    return (factor * r[:, :128] - (factor * factor) * rows_bf.astype(f32) * r[:, 128:]).astype(bf16)


def weight_parts(step, steps, lhs_ref, pg_ref, keep_ref, send_ref, width):
    own = width // 2
    for xr in range(2):

        @pl.when(step == steps + xr)
        def _():
            rhs = [pg_ref[:, pl.ds(c * width + half_cols(xr, own), own)] for c in range(pg_ref.shape[1] // width)]
            put_grad(keep_ref, send_ref, mm(lhs_ref[...], jnp.concatenate(rhs, axis=1)))


def key_back(
    len_ref, kv_ref, tok_ref, map_ref, own_ref, tot_ref, span_ref, recv_ref,
    vec_in, *refs,
    half, nseg, heads, hdim, steps, dp_count, sort, row
):
    pgo_ref, vec_ref, keep_ref, send_ref, sg_ref, sgt_ref, mapg_ref, pg_ref, lhs_ref, tmp_ref = refs[-10:]
    step = pl.program_id(0)
    rows, width = tok_ref.shape
    feat = map_ref.shape[2]
    wide = nseg * hdim
    starts, ends = bounds(len_ref, nseg)
    here = spanning(ends, half)
    first = lax.axis_index("x") * half + step * rows
    factor = hdim ** (-0.25)

    @pl.when(step == 0)
    def _():
        vec_ref[...] = vec_in[...]
        put_states(own_ref, tot_ref, span_ref, recv_ref, sg_ref, sgt_ref, here, nseg, heads, hdim)
        map_back(map_ref, mapg_ref, heads, hdim)

    @pl.when(step < steps)
    def _():
        at = pl.multiple_of(step * rows, 128)
        mine = pl.ds(at, rows)
        seg_wide, seg8 = seg_masks(first, rows, hdim, nseg, starts, ends)
        seg_wide_bf, seg8_bf = as_bf(seg_wide), as_bf(seg8)
        low_half = iota((rows, 128), 1) < hdim
        for p in range(heads // 2):
            k_cols, v_cols = slice(128 * p, 128 * (p + 1)), slice(width + 128 * p, width + 128 * (p + 1))
            k_pair = kv_ref[:, k_cols]
            v_reps = replicate(kv_ref[:, v_cols], low_half, hdim)
            logs, folded = [], []
            for j in range(2):
                h = 2 * p + j
                logits = factor * mm(k_pair, head_map(map_ref, h)) - (0.5 * factor * factor) * key_offset(k_pair, low_half, j)
                feats = jnp.exp(logits)
                lhs = jnp.concatenate([v_reps[j]] * 2, axis=1) * seg_wide_bf
                state_grad = sg_ref[wide * h : wide * (h + 1), :]
                slope = mm(lhs, state_grad) + mm(seg8_bf, sgt_ref[:, feat * h : feat * (h + 1)])
                logs.append((slope * feats).astype(bf16))
                r = jnp.where(seg_wide, mm_nt(feats.astype(bf16), state_grad), 0.0)
                folded.append(r[:, :128] + r[:, 128:])
            pg_ref[mine, k_cols] = rows_grad(logs, mapg_ref[p], k_pair, factor)
            pg_ref[mine, v_cols] = fold_pair(folded, low_half, hdim).astype(bf16)
        grads = pg_ref[mine, :]
        pgo_ref[...] = grads
        add_row(vec_ref, row + 1, grads[:, :width].astype(f32))
        add_row(vec_ref, row + 2, grads[:, width:].astype(f32))
        put_transposed(lhs_ref, tmp_ref, tok_ref[...], at, row_sources(dp_count) if sort else [])

    weight_parts(step, steps, lhs_ref, pg_ref, keep_ref, send_ref, width)


def query_back(
    len_ref, q_ref, num_ref, dgm_ref, tok_ref, map_ref, own_ref, tot_ref, span_ref, recv_ref,
    vec_in, *refs,
    half, nseg, heads, hdim, steps, dp_count, sort, row
):
    pgo_ref, vec_ref, keep_ref, send_ref, st_ref, totp_ref, mapg_ref, pg_ref, lhs_ref, tmp_ref = refs[-10:]
    step = pl.program_id(0)
    rows, width = tok_ref.shape
    feat = map_ref.shape[2]
    wide = nseg * hdim
    starts, ends = bounds(len_ref, nseg)
    first = lax.axis_index("x") * half + step * rows
    factor = hdim ** (-0.25)

    @pl.when(step == 0)
    def _():
        vec_ref[...] = vec_in[...]
        put_states(own_ref, tot_ref, span_ref, recv_ref, st_ref, totp_ref, spanning(ends, half), nseg, heads, hdim)
        map_back(map_ref, mapg_ref, heads, hdim)

    @pl.when(step < steps)
    def _():
        at = pl.multiple_of(step * rows, 128)
        mine = pl.ds(at, rows)
        seg_wide, _ = seg_masks(first, rows, hdim, nseg, starts, ends)
        seg_wide_bf = as_bf(seg_wide)
        low_half = iota((rows, 128), 1) < hdim
        den_m = dgm_ref[...]
        for p in range(heads // 2):
            cols = slice(128 * p, 128 * (p + 1))
            q_pair = q_ref[:, cols]
            reps = replicate(num_ref[:, cols], low_half, hdim)
            logs = []
            for j in range(2):
                h = 2 * p + j
                proj = mm(q_pair, head_map(map_ref, h))
                shifted = proj - jnp.max(proj, axis=-1, keepdims=True)
                lhs = jnp.concatenate([reps[j]] * 2, axis=1) * seg_wide_bf
                slope = mm(lhs, st_ref[wide * h : wide * (h + 1), :]) + mm(den_m, totp_ref[:, feat * h : feat * (h + 1)])
                slope = slope * jnp.exp(factor * shifted)
                peak = jnp.where(shifted == 0.0, 1.0, 0.0)
                share = jnp.sum(slope, axis=-1, keepdims=True) / jnp.sum(peak, axis=-1, keepdims=True)
                logs.append((slope - peak * share).astype(bf16))
            pg_ref[mine, cols] = rows_grad(logs, mapg_ref[p], q_pair, factor)
        grads = pg_ref[mine, :]
        pgo_ref[...] = grads
        add_row(vec_ref, row, grads.astype(f32))
        put_transposed(lhs_ref, tmp_ref, tok_ref[...], at, row_sources(dp_count) if sort else [])

    weight_parts(step, steps, lhs_ref, pg_ref, keep_ref, send_ref, width)


def token_grads(agrad_ref, pgq_ref, pgkv_ref, wq_ref, wk_ref, wv_ref, *refs):
    out_ref = refs[-1]
    width = agrad_ref.shape[1]
    total = agrad_ref[...].astype(f32) + mm_nt(pgq_ref[...], wq_ref[...])
    total += mm_nt(pgkv_ref[:, :width], wk_ref[...])
    out_ref[...] = (total + mm_nt(pgkv_ref[:, width:], wv_ref[...])).astype(bf16)


def params(micros):
    return dict(
        compiler_params=pltpu.CompilerParams(vmem_limit_bytes=vmem_limit),
        cost_estimate=pl.CostEstimate(flops=int(micros * 1.1e9), bytes_accessed=int(micros * 1e6), transcendentals=0),
    )


def whole(shape):
    return pl.BlockSpec(shape, lambda i: (0,) * len(shape), pipeline_mode=pl.Buffered(1))


def resident(shape):
    return pl.BlockSpec(shape, lambda i: (0,) * len(shape))


def sds(shape, dtype):
    return jax.ShapeDtypeStruct(shape, dtype)


every_axis = ("z", "y", "c", "x")


def exchange(values, mask, dp_count):
    return lax.ppermute(values, every_axis, [(i, i ^ mask) for i in range(2 * dp_count)])


def sort_rows(keep, send, dp_count):
    _, _, blocks, quarter, _ = keep.shape
    natural = jnp.stack([keep, send]).transpose(0, 1, 4, 2, 3, 5).reshape(dp_count, -1, 2, blocks, 128)
    rows = jnp.take(natural, jnp.stack(row_sources(dp_count)), axis=0)
    rows = rows.reshape(2, 2, quarter, 2, blocks, 128).transpose(0, 1, 3, 4, 2, 5)
    return rows[0], rows[1]


def route(name, arrays, outs, moves, vec=None, after=()):
    rows = arrays[0].shape[-2]
    grid = 2 if rows % 32 == 0 else 1
    own, got, send = vec if vec is not None else (None, None, None)
    extra = [own] if vec is not None else []
    if vec is not None:
        count, blocks = own.shape[0], own.shape[1] // 128
        assert grid == 2 and 2 * count * blocks == rows

    def spec(shape):
        lead = len(shape) - 2
        return pl.BlockSpec(tuple(shape[:lead]) + (rows // grid, 128), lambda i: (0,) * lead + (i, 0))

    def kernel(*refs):
        ins, results = refs[: len(arrays)], refs[len(arrays) + len(extra) + len(after) :]
        for out, to, parts in moves:
            total = ins[parts[0][0]][parts[0][1]].astype(f32)
            for n, at in parts[1:]:
                total = total + ins[n][at].astype(f32)
            results[out][to] = total.astype(bf16)
        if vec is not None:
            step = pl.program_id(0)
            sums_ref = results[-1]

            @pl.when(step == 0)
            def _():
                sums_ref[...] = refs[len(arrays)][...]

            if got is not None:
                other = ins[got[0]][got[1]].astype(f32)
                sums_ref[...] += jnp.concatenate([other[b * count : (b + 1) * count] for b in range(blocks)], axis=1)
            if send is not None:
                sums = sums_ref[...]
                hi = sums.astype(bf16)
                part = jnp.where(step == 0, hi.astype(f32), sums - hi.astype(f32)).astype(bf16)
                rows_of = [part[:, 128 * b : 128 * (b + 1)] for b in range(blocks)]
                results[send[0]][send[1]] = jnp.concatenate(rows_of, axis=0)

    shapes = [sds(v, bf16) for v in outs]
    specs = [spec(v) for v in outs]
    if vec is not None:
        shapes.append(sds(own.shape, f32))
        specs.append(resident(own.shape))
    return pl.pallas_call(
        kernel,
        name=name,
        grid=(grid,),
        in_specs=[spec(a.shape) for a in arrays] + [resident(v.shape) for v in extra] + [pl.BlockSpec(memory_space=pl.ANY)] * len(after),
        out_specs=specs,
        out_shape=shapes,
        **params(3),
    )(*arrays, *extra, *after)


def first_moves(groups, left):
    moves, n = [], 0
    for array, blocks in groups:
        for b in range(blocks):
            for y in range(2):
                for x in range(2):
                    parts = [(array, (y, x, b)), (array + 1, (y, x, b))]
                    moves.append((x, (y, n), parts) if n < left else (2 + y, (x, n - left), parts))
            n += 1
    return moves


def second_moves(array, left, right, out):
    moves = []
    for b in range(left):
        moves += [(out if y == 0 else out + 1, (b,), [(array, (y, b)), (array + 1, (y, b))]) for y in range(2)]
    for b in range(right):
        moves += [(out if x == 0 else out + 2, (left + b if x == 0 else b,), [(array + 2, (x, b)), (array + 3, (x, b))]) for x in range(2)]
    return moves


def third_sum(keep, left_got, right_got):
    return added(bf16, keep, jnp.concatenate([left_got, right_got], axis=0))


def added(dtype, *parts):
    return functools.reduce(jnp.add, [p.astype(f32) for p in parts]).astype(dtype)


def odd_even(part, count):
    pairs = part.reshape(part.shape[0], count // 2, 2, -1, 128)
    return [pairs[:, :, k].reshape(part.shape[0], -1, 128) for k in range(2)]


def columns(part):
    return part.transpose(1, 0, 2).reshape(part.shape[1], -1)


def body(
    tokens, lengths, feature_map, qkv_weight, qkv_bias, out_weight, out_bias, ln1_gain, ln1_shift,
    up_weight, up_bias, down_weight, down_bias, ln2_gain, ln2_shift, cotangent,
):
    half, width = tokens.shape
    heads, hdim, feat = feature_map.shape
    nseg = lengths.shape[1]
    hidden_units = up_weight.shape[1]
    wide = nseg * hdim
    dp_count = lax.axis_size(("z", "y", "c"))
    assert lax.axis_size("x") == 2 and dp_count & (dp_count - 1) == 0 and dp_count >= 8
    assert 2 * hdim == 128 and wide == 256 and 8 * heads <= 128
    sort = (width // dp_count) % 16 == 0
    layout = dict(dp_count=dp_count, sort=sort)
    by_part = qkv_weight.transpose(1, 0, 2)
    rows = min(256, half)
    steps = half // rows
    big = min(512, half)
    big_steps = half // big
    span_rows = heads * hdim + 16
    state_shapes = [
        sds((heads * wide, feat), bf16), sds((heads * 8, feat), f32),
        sds((span_rows - 16, feat), f32), sds((span_rows, feat), bf16),
    ]
    state_specs = [resident(s.shape) for s in state_shapes]
    lens = pl.BlockSpec(memory_space=pltpu.SMEM)
    acc = pltpu.VMEM((heads, wide + 16, feat), f32)
    features = whole(feature_map.shape)
    square = whole((width, width))
    w_specs = [pl.BlockSpec((None, width, width), lambda i, c=c: (c, 0, 0), pipeline_mode=pl.Buffered(1)) for c in range(3)]

    def tile(cols):
        return pl.BlockSpec((rows, cols), lambda i: (jnp.minimum(i, steps - 1), 0))

    def vector(size):
        return pl.BlockSpec((size,), lambda i: (0,))

    static = dict(half=half, nseg=nseg, heads=heads, hdim=hdim)
    dense = 2 * half * width

    def parts(cols, before, count):
        shape = sds((2, 2, cols // 128, width // 4, 128), bf16)
        at = lambda i: (0, jnp.maximum(i - before, 0) // count, 0, 0, 0)
        return [pl.BlockSpec((2, 1, cols // 128, width // 4, 128), at)] * 2, [shape] * 2

    def run(kernel, name, grid, in_specs, args, after, **more):
        fence = [pl.BlockSpec(memory_space=pl.ANY)] * len(after)
        return pl.pallas_call(kernel, name=name, grid=grid, in_specs=list(in_specs) + fence, **more)(*args, *after)

    def over_core(keep, send):
        if not sort:
            keep, send = sort_rows(keep, send, dp_count)
        return keep, exchange(send, 2, dp_count)

    kv, own, tot, span, send = pl.pallas_call(
        functools.partial(forward_keys, **static),
        name="key_states",
        grid=(steps,),
        in_specs=[lens, tile(width), w_specs[1], w_specs[2], whole((3, width)), features],
        out_specs=[tile(2 * width)] + state_specs,
        out_shape=[sds((half, 2 * width), bf16)] + state_shapes,
        scratch_shapes=[acc],
        **params(12),
    )(lengths, tokens, by_part, by_part, qkv_bias, feature_map)
    recv = exchange(send, 1, dp_count)
    q_rows, q_feats = pl.pallas_call(
        functools.partial(forward_queries, heads=heads, hdim=hdim),
        name="query_features",
        grid=(steps,),
        in_specs=[tile(width), w_specs[0], whole((3, width)), features],
        out_specs=[tile(width), tile(heads * feat)],
        out_shape=[sds((half, width), bf16), sds((half, heads * feat), bf16)],
        **params(7),
    )(tokens, by_part, qkv_bias, feature_map)

    chunk = 512
    count = hidden_units // chunk
    half_w, half_u = width // 2, hidden_units // 2
    sum_at = 6 + hidden_units // width
    vec_rows = 16
    assert sum_at + 3 <= vec_rows and 2 * vec_rows * width // 128 == width // 4

    def tiles(cols, size, before):
        per = cols // size

        def at(i):
            t = jnp.clip(i - before, 0, 2 * per - 1)
            return (0, t // per, t % per, 0, 0)

        shape = sds((2, 2, cols // 128, width // 4, 128), bf16)
        return [pl.BlockSpec((2, 1, size // 128, width // 4, 128), at)] * 2, [shape] * 2

    d_specs, d_shapes = tiles(half_u, chunk, big_steps)
    hbm = pl.BlockSpec(memory_space=pl.ANY)

    def big_tile(cols):
        return pl.BlockSpec((big, cols), lambda i: (jnp.minimum(i, big_steps - 1), 0))

    tile_cols = (width, width, width, 128, width, width)
    (output, agrad, num_grad, den_m, normed, mixed, ugrad, vec, s_own, s_tot, s_span, s_send, d_keep, d_send) = run(
        functools.partial(chain, chunk=chunk, steps=big_steps, **layout, **static),
        "chain",
        (big_steps + count,),
        [lens, big_tile(width), big_tile(heads * feat), big_tile(width)]
        + [hbm] + [whole(v.shape) for v in (tot, span, recv)]
        + [square, vector(width), vector(width), vector(width)]
        + [hbm, vector(hidden_units), hbm]
        + [vector(width)] * 3,
        (
            lengths, tokens, q_feats, cotangent, own, tot, span, recv, out_weight, out_bias, ln1_gain, ln1_shift,
            up_weight, up_bias, down_weight, down_bias, ln2_gain, ln2_shift,
        ),
        (),
        out_specs=[big_tile(c) for c in tile_cols] + [hbm, whole((vec_rows, width))] + [whole(v.shape) for v in state_shapes] + d_specs,
        out_shape=[sds((half, c), bf16) for c in tile_cols + (hidden_units,)] + [sds((vec_rows, width), f32)] + state_shapes + d_shapes,
        scratch_shapes=[
            pltpu.VMEM((heads * wide, feat), bf16),
            pltpu.VMEM((128, heads * feat), bf16),
            pltpu.VMEM((256, width + 128), bf16),
            pltpu.VMEM((2 * width, 128), bf16),
            acc,
            pltpu.VMEM((half, hidden_units), bf16),
            pltpu.VMEM((big, hidden_units), bf16),
            pltpu.VMEM((width, half), bf16),
            pltpu.VMEM((width, big // 2), bf16),
            pltpu.VMEM(up_weight.shape, bf16),
            pltpu.VMEM(down_weight.shape, bf16),
            pltpu.SemaphoreType.DMA((5,)),
        ],
        **params(58),
    )
    s_recv = exchange(s_send, 1, dp_count)
    d_keep, d_got = over_core(d_keep, d_send)
    u_specs, u_shapes = tiles(half_u, chunk, 0)
    o_specs, o_shapes = tiles(half_w, half_w, count)
    whole_rows = whole((half, width))
    u_keep, u_send, o_keep, o_send = run(
        functools.partial(up_out_grads, count=count, **layout),
        "up_out_grads",
        (count + 2,),
        [whole_rows] * 3 + [pl.BlockSpec((half, chunk), lambda i: (0, jnp.minimum(i, count - 1)))],
        (normed, agrad, mixed, ugrad),
        (),
        out_specs=u_specs + o_specs,
        out_shape=u_shapes + o_shapes,
        scratch_shapes=[pltpu.VMEM((width, half), bf16)] * 3,
        **params(9),
    )
    u_keep, u_got = over_core(u_keep, u_send)
    o_keep, o_got = over_core(o_keep, o_send)
    block = (width // 4, 128)
    d_n, u_n, o_n = half_u // 128, half_u // 128, half_w // 128
    d_l, uo_l, qkv_n, qkv_l = d_n // 2, (u_n + o_n) // 2, 3 * o_n, 3 * o_n // 2
    d_r, uo_r, qkv_r = d_n - d_l, u_n + o_n - uo_l, qkv_n - qkv_l
    pair = lambda n: (2, n) + block
    d_lk, d_ls, d_rk, d_rs = route("down_1", [d_keep, d_got], [pair(d_l)] * 2 + [pair(d_r)] * 2, first_moves([(0, d_n)], d_l), None, (u_keep, s_recv))
    x_got, y_got = exchange(d_ls, 1, dp_count), exchange(d_rs, 4, dp_count)
    rows = min(512, half)
    steps = half // rows

    def back_scratch(n):
        return [
            pltpu.VMEM((heads // 2, 4 * hdim, 2 * feat), bf16),
            pltpu.VMEM((half, n * width), bf16),
            pltpu.VMEM((width, half), bf16),
            pltpu.VMEM((width, rows), bf16),
        ]

    q_specs, q_shapes = parts(half_w, steps, 1)
    state_scratch = [pltpu.VMEM((heads * wide, feat), bf16), pltpu.VMEM((128, heads * feat), bf16)]
    sums = resident((vec_rows, width))
    sums_shape = sds((vec_rows, width), f32)
    pg_q, vec, q_keep, q_send = run(
        functools.partial(query_back, steps=steps, row=sum_at, **layout, **static),
        "query_back",
        (steps + 2,),
        [lens, tile(width), tile(width), tile(128), tile(width), features] + [whole(v.shape) for v in (own, tot, span, recv)] + [sums],
        (lengths, q_rows, num_grad, den_m, tokens, feature_map, own, tot, span, recv, vec),
        (d_lk,),
        out_specs=[tile(width), sums] + q_specs,
        out_shape=[sds((half, width), bf16), sums_shape] + q_shapes,
        scratch_shapes=state_scratch + back_scratch(1),
        **params(18),
    )
    q_keep, q_got = over_core(q_keep, q_send)
    arrays = [d_lk, x_got, d_rk, y_got, u_keep, u_got, o_keep, o_got]
    moves = second_moves(0, d_l, d_r, 0)
    shift = {1: 4, 2: 3}
    moves = [(shift.get(out, out), at, terms) for out, at, terms in moves]
    for out, at, terms in first_moves([(4, u_n), (6, o_n)], uo_l):
        place = at[0] * (uo_l if out < 2 else uo_r) + at[1]
        if out in (0, 2):
            moves.append((1 if out == 0 else 2, at, terms))
        else:
            moves.append((3, (d_r + place,), terms) if out == 1 else (4, (d_l + place,), terms))
    flat = lambda n: (n,) + block
    d_part, uo_lk, uo_rk, x_send, y_send = route(
        "down_2_up_1", arrays, [flat(d_n), pair(uo_l), pair(uo_r), flat(d_r + 2 * uo_l), flat(d_l + 2 * uo_r)], moves
    )
    x_got, y_got = exchange(x_send, 1, dp_count), exchange(y_send, 4, dp_count)

    kv_specs, kv_shapes = parts(2 * half_w, steps, 1)
    pg_kv, vec, kv_keep, kv_send = run(
        functools.partial(key_back, steps=steps, row=sum_at, **layout, **static),
        "key_back",
        (steps + 2,),
        [lens, tile(2 * width), tile(width), features] + [whole(v.shape) for v in (s_own, s_tot, s_span, s_recv)] + [sums],
        (lengths, kv, tokens, feature_map, s_own, s_tot, s_span, s_recv, vec),
        (d_part,),
        out_specs=[tile(2 * width), sums] + kv_specs,
        out_shape=[sds((half, 2 * width), bf16), sums_shape] + kv_shapes,
        scratch_shapes=state_scratch + back_scratch(2),
        **params(18),
    )
    kv_keep, kv_got = over_core(kv_keep, kv_send)
    vec_got = exchange(vec, 2, dp_count)
    moves = []
    for out, at, terms in second_moves(3, uo_l, uo_r, 0):
        placed = []
        for n, index in terms:
            if n == 4:
                n, index = 1, (d_r + index[0] * uo_l + index[1],)
            elif n == 6:
                n, index = 2, (d_l + index[0] * uo_r + index[1],)
            elif n == 5:
                n = 4
            placed.append((n, index))
        moves.append((out, at, placed))
    d_x, d_y = x_got[:d_r], y_got[:d_l]
    uo_part, uo_ls, uo_rs = route(
        "up_2", [d_part, x_got, y_got, uo_lk, uo_rk], [flat(uo_l + uo_r), flat(uo_l), flat(uo_r)], moves
    )
    x_got, y_got = exchange(uo_rs, 1, dp_count), exchange(uo_ls, 4, dp_count)
    z_bits = [8 << b for b in range((dp_count // 4).bit_length() - 1)]
    left_z = [dp_count // 4 >> n for n in range(len(z_bits))]

    def start_z(part, n):
        keep, send = odd_even(part, left_z[n])
        return keep, exchange(send, z_bits[n], dp_count)

    def end_z(keep, got, n):
        return added(bf16 if n + 1 < len(z_bits) else f32, keep, got)

    down_z = start_z(third_sum(d_part, d_y, d_x), 0)
    qkv_lk, qkv_ls, qkv_rk, qkv_rs, vec = route(
        "qkv_1",
        [q_keep, q_got, kv_keep, kv_got],
        [pair(qkv_l), flat(2 * qkv_l + 1), pair(qkv_r), pair(qkv_r)],
        [
            (out, (at[0] * qkv_l + at[1],) if out == 1 else at, terms)
            for out, at, terms in first_moves([(0, o_n), (2, 2 * o_n)], qkv_l)
        ],
        (vec + vec_got, None, (1, (2 * qkv_l,))),
        (uo_part,),
    )
    qkv_x, qkv_y = exchange(qkv_ls, 1, dp_count), exchange(qkv_rs, 4, dp_count)

    grad_tokens = run(
        token_grads,
        "token_grads",
        (steps,),
        [tile(width), tile(width), tile(2 * width)] + w_specs,
        (agrad, pg_q, pg_kv, by_part, by_part, by_part),
        (qkv_lk, down_z[0]),
        out_specs=tile(width),
        out_shape=sds((half, width), bf16),
        **params(8),
    )
    up_z = start_z(third_sum(uo_part, y_got, x_got), 0)
    down_part = end_z(*down_z, 0)
    if len(z_bits) > 1:
        down_z = start_z(down_part, 1)
    moves = []
    for out, at, terms in second_moves(0, qkv_l, qkv_r, 0):
        terms = [(n, (at_n[0] * qkv_l + at_n[1],) if n == 1 else at_n) for n, at_n in terms]
        moves.append((out, at, terms))
    qkv_part, qkv_ls, qkv_rs, vec = route(
        "qkv_2",
        [qkv_lk, qkv_x, qkv_rk, qkv_y],
        [flat(qkv_n), flat(qkv_l + 1), flat(qkv_r)],
        moves,
        (vec, (1, (2 * qkv_l,)), (1, (qkv_l,))),
        (up_z[0], down_z[0], grad_tokens),
    )
    qkv_x, qkv_y = exchange(qkv_rs, 1, dp_count), exchange(qkv_ls, 4, dp_count)

    def rest(part, z, first):
        for n in range(first, len(z_bits)):
            part = end_z(*z, n)
            if n + 1 < len(z_bits):
                z = start_z(part, n + 1)
        return columns(part)

    d_down = rest(down_part, down_z, 1) if len(z_bits) > 1 else columns(down_part)
    d_up_out = rest(None, up_z, 0)

    def add_vec(vec, got):
        count, blocks = vec.shape[0], vec.shape[1] // 128
        got = got.reshape(-1, 128).astype(f32)
        got = got[: count * blocks] + got[count * blocks :]
        return vec + jnp.concatenate([got[b * count : (b + 1) * count] for b in range(blocks)], axis=1)

    def vec_rows_of(vec):
        hi = vec.astype(bf16)
        lo = (vec - hi.astype(f32)).astype(bf16)
        return jnp.concatenate([v[:, 128 * b : 128 * (b + 1)] for v in (hi, lo) for b in range(vec.shape[1] // 128)], axis=0)

    vec = add_vec(vec, qkv_y[qkv_l])
    part = third_sum(qkv_part, qkv_y[:qkv_l], qkv_x)
    for n, bit in enumerate(z_bits):
        keep, send = odd_even(part, left_z[n])
        got = exchange(jnp.concatenate([send.reshape(-1, 128), vec_rows_of(vec)], axis=0), bit, dp_count)
        size = send.size // 128
        vec = add_vec(vec, got[size:])
        part = end_z(keep, got[:size].reshape(send.shape), n)
    d_qkv = part.reshape(3, o_n, -1, 128).transpose(2, 0, 1, 3).reshape(-1, 3, half_w)
    return (
        output,
        grad_tokens,
        d_qkv,
        vec[sum_at : sum_at + 3],
        d_up_out[:, half_u:],
        vec[3],
        vec[4],
        vec[5],
        d_up_out[:, :half_u],
        vec[6:sum_at].reshape(-1),
        d_down,
        vec[0],
        vec[1],
        vec[2],
    )


def solution(mesh):
    dp_count = mesh.shape["dp"]
    fine = jax.sharding.Mesh(mesh.devices.reshape(dp_count // 4, 2, 2, 2), every_axis)
    dp = ("z", "y", "c")
    rows = P(every_axis, None)
    in_specs = (rows, P(dp, None)) + (P(),) * 13 + (rows,)
    out_specs = (
        rows, rows, P(dp, None, "x"), P(), P(dp, "x"), P(), P(), P(),
        P(dp, "x"), P(), P(dp, "x"), P(), P(), P(),
    )
    return jax.shard_map(body, mesh=fine, in_specs=in_specs, out_specs=out_specs, check_vma=False)
```

```python
import functools

import jax
import jax.numpy as jnp
from jax import lax
from jax.experimental import pallas as pl
from jax.experimental.pallas import tpu as pltpu
from jax.sharding import PartitionSpec as P

bf16 = jnp.bfloat16
f32 = jnp.float32
norm_epsilon = 1e-06
root_half = 0.7071067811865476
inv_root_tau = 0.3989422804014327
vmem_limit = 62 * 1024 * 1024
stream_lead = 6
nt_dims = (((1,), (1,)), ((), ()))


def mm(a, b):
    return jnp.dot(a, b, preferred_element_type=f32)


def mm_nt(a, b):
    return lax.dot_general(a, b, nt_dims, preferred_element_type=f32)


def iota(shape, dim):
    return lax.broadcasted_iota(jnp.int32, shape, dim)


def bounds(len_ref, nseg):
    starts, ends, run = [], [], jnp.int32(0)
    for s in range(nseg):
        starts.append(run)
        run = run + len_ref[0, s]
        ends.append(run)
    return starts, ends


def spanning(ends, half):
    count = jnp.int32(0)
    for end in ends:
        count = count + (end < half).astype(jnp.int32)
    return count


def pick(index, values):
    out = jnp.full(index.shape, values[-1], jnp.int32)
    for s in range(len(values) - 2, -1, -1):
        out = jnp.where(index == s, values[s], out)
    return out


def inside(pos, index, starts, ends):
    return jnp.logical_and(pos >= pick(index, starts), pos < pick(index, ends))


def as_bf(mask):
    return jnp.where(mask, 1.0, 0.0).astype(bf16)


def split_hi_lo(v):
    hi = v.astype(bf16)
    lo = (v - hi.astype(f32)).astype(bf16)
    return jnp.concatenate([hi, lo], axis=1)


def masked_rows(rows_t, lane_masks, tail):
    return jnp.concatenate([rows_t * m for m in lane_masks] + [tail], axis=0)


def head_map(map_ref, h):
    m = map_ref[h]
    z = jnp.zeros_like(m)
    return jnp.concatenate([m, z] if h % 2 == 0 else [z, m], axis=0)


def key_offset(k_pair, low_half, j):
    sq = jnp.square(k_pair.astype(f32))
    mine = low_half if j == 0 else jnp.logical_not(low_half)
    return jnp.sum(jnp.where(mine, sq, 0.0), axis=-1, keepdims=True)


def put_states(own_ref, tot_ref, span_ref, recv_ref, st_ref, totp_ref, here, nseg, heads, hdim):
    wide = nseg * hdim
    feat = st_ref.shape[1]
    recv_tot = recv_ref[heads * hdim :, :].astype(f32)
    seg_row = iota((8, feat), 0)
    for h in range(heads):
        if own_ref is not None:
            st_ref[h * wide : (h + 1) * wide, :] = own_ref[h * wide : (h + 1) * wide, :]
        both = span_ref[h * hdim : (h + 1) * hdim, :] + recv_ref[h * hdim : (h + 1) * hdim, :].astype(f32)
        at = pl.multiple_of(h * wide + here * hdim, hdim)
        st_ref[pl.ds(at, hdim), :] = both.astype(bf16)
        tot = tot_ref[8 * h : 8 * h + 8, :]
        tot = jnp.where(seg_row == here, tot + recv_tot[h : h + 1, :], tot)
        parts = [tot]
        if h > 0:
            parts.insert(0, jnp.zeros((8 * h, feat), f32))
        if 8 * h + 8 < 128:
            parts.append(jnp.zeros((128 - 8 * h - 8, feat), f32))
        totp_ref[:, feat * h : feat * (h + 1)] = jnp.concatenate(parts, axis=0).astype(bf16)


def emit_states(acc_ref, own_ref, tot_ref, span_ref, send_ref, here, nseg, heads, hdim):
    wide = nseg * hdim
    feat = acc_ref.shape[2]
    for h in range(heads):
        own_ref[h * wide : (h + 1) * wide, :] = acc_ref[h, 0:wide, :].astype(bf16)
        tot_ref[8 * h : 8 * h + 8, :] = acc_ref[h, wide : wide + 8, :]
        at = pl.multiple_of(here * hdim, hdim)
        part = acc_ref[h, pl.ds(at, hdim), :]
        span_ref[h * hdim : (h + 1) * hdim, :] = part
        send_ref[h * hdim : (h + 1) * hdim, :] = part.astype(bf16)
    row = iota((16, feat), 0)
    seg_row = iota((8, feat), 0)
    tots = jnp.zeros((16, feat), f32)
    for h in range(heads):
        mine = jnp.sum(jnp.where(seg_row == here, acc_ref[h, wide : wide + 8, :], 0.0), axis=0, keepdims=True)
        tots = jnp.where(row == h, mine, tots)
    send_ref[heads * hdim :, :] = tots.astype(bf16)


def lane_segment_masks(first, rows, hdim, starts, ends):
    pos = first + iota((hdim, rows), 1)
    masks = [as_bf(jnp.logical_and(pos >= a, pos < b)) for a, b in zip(starts, ends)]
    pos = first + iota((16, rows), 1)
    seg = iota((16, rows), 0)
    tail = as_bf(jnp.logical_and(seg < len(starts), inside(pos, seg, starts, ends)))
    return masks, tail


def seg_masks(first, rows, hdim, nseg, starts, ends):
    pos = first + iota((rows, nseg * hdim), 0)
    wide = inside(pos, iota((rows, nseg * hdim), 1) >> (hdim.bit_length() - 1), starts, ends)
    lane8 = iota((rows, 128), 1) & 7
    pos = first + iota((rows, 128), 0)
    eight = jnp.logical_and(lane8 < nseg, inside(pos, lane8, starts, ends))
    return wide, eight


def block_of(p, dp_count):
    top = dp_count.bit_length() - 1
    return (p >> (top - 1)) & 1 | ((p >> (top - 2)) & 1) << 1 | (p & (dp_count // 4 - 1)) << 2


def dp_index():
    return (lax.axis_index("z") * 2 + lax.axis_index("y")) * 2 + lax.axis_index("c")


def row_sources(dp_count):
    return [jnp.bitwise_xor(dp_index(), block_of(p, dp_count)) for p in range(dp_count)]


def put_transposed(lhs_ref, tmp_ref, values, at, sources):
    rows, width = values.shape
    cols = pl.ds(at, rows)
    if not sources:
        lhs_ref[:, cols] = values.T
        return
    block = width // len(sources)
    tmp_ref[...] = values.T
    for p, source in enumerate(sources):
        lhs_ref[p * block : (p + 1) * block, cols] = tmp_ref[pl.ds(pl.multiple_of(source * block, 16), block), :]


def fold_pair(folded, low_half, hdim):
    straight = jnp.where(low_half, folded[0], folded[1])
    crossed = jnp.where(low_half, folded[1], folded[0])
    return straight + pltpu.roll(crossed, hdim, 1)


def forward_keys(
    len_ref, tok_ref, wk_ref, wv_ref, b_ref, map_ref, kv_ref, own_ref, tot_ref, span_ref, send_ref, acc_ref,
    *, half, nseg, heads, hdim
):
    step = pl.program_id(0)
    rows, width = tok_ref.shape
    starts, ends = bounds(len_ref, nseg)
    here = spanning(ends, half)
    first = lax.axis_index("x") * half + step * rows
    factor = hdim ** (-0.25)

    @pl.when(step == 0)
    def _():
        acc_ref[...] = jnp.zeros_like(acc_ref)

    masks, tail = lane_segment_masks(first, rows, hdim, starts, ends)
    tok = tok_ref[...]
    keys = (mm(tok, wk_ref[...]) + b_ref[1:2, :]).astype(bf16)
    vals = (mm(tok, wv_ref[...]) + b_ref[2:3, :]).astype(bf16)
    kv_ref[:, :width] = keys
    kv_ref[:, width:] = vals
    low_half = iota((rows, 128), 1) < hdim
    for p in range(heads // 2):
        k_pair = keys[:, 128 * p : 128 * (p + 1)]
        v_t = vals[:, 128 * p : 128 * (p + 1)].T
        for j in range(2):
            h = 2 * p + j
            logits = factor * mm(k_pair, head_map(map_ref, h)) - (0.5 * factor * factor) * key_offset(k_pair, low_half, j)
            feats = jnp.exp(logits).astype(bf16)
            lhs = masked_rows(v_t[j * hdim : (j + 1) * hdim, :], masks, tail)
            acc_ref[h] += mm(lhs, feats)

    @pl.when(step == pl.num_programs(0) - 1)
    def _():
        emit_states(acc_ref, own_ref, tot_ref, span_ref, send_ref, here, nseg, heads, hdim)


def forward_queries(tok_ref, wq_ref, b_ref, map_ref, q_ref, qf_ref, *, heads, hdim):
    feat = map_ref.shape[2]
    factor = hdim ** (-0.25)
    queries = (mm(tok_ref[...], wq_ref[...]) + b_ref[0:1, :]).astype(bf16)
    q_ref[...] = queries
    for h in range(heads):
        proj = mm(queries[:, 128 * (h // 2) : 128 * (h // 2 + 1)], head_map(map_ref, h))
        top = jnp.max(proj, axis=-1, keepdims=True)
        qf_ref[:, feat * h : feat * (h + 1)] = jnp.exp(factor * (proj - top)).astype(bf16)


def norm_backward(incoming, scaled, inverse, gain):
    weighted = incoming * gain
    return inverse * (
        weighted
        - jnp.mean(weighted, axis=-1, keepdims=True)
        - scaled * jnp.mean(weighted * scaled, axis=-1, keepdims=True)
    )


def norm_parts(values):
    centred = values - jnp.mean(values, axis=-1, keepdims=True)
    spread = jnp.mean(centred * centred, axis=-1, keepdims=True)
    inverse = lax.rsqrt(spread + norm_epsilon)
    return centred * inverse, inverse


def gelu_parts(u):
    cdf = 0.5 + 0.5 * lax.erf(u * root_half)
    return u * cdf, cdf + u * (inv_root_tau * jnp.exp(-0.5 * (u * u)))


def flat_row(ref):
    return ref[...].reshape(1, -1)


def add_row(vec_ref, row, values):
    vec_ref[row : row + 1, :] += jnp.sum(values, axis=0, keepdims=True)


def put_grad(keep_ref, send_ref, grad):
    quarter = grad.shape[0] // 4
    for b in range(grad.shape[1] // 128):
        cols = slice(128 * b, 128 * (b + 1))
        for y in range(2):
            keep_ref[y, 0, b] = grad[y * quarter : (y + 1) * quarter, cols].astype(bf16)
            send_ref[y, 0, b] = grad[(2 + y) * quarter : (3 + y) * quarter, cols].astype(bf16)


def half_cols(xr, half_width):
    x = lax.axis_index("x")
    return pl.multiple_of(jnp.bitwise_xor(x, xr) * half_width, 128)


def interleave(first, second, lead):
    alive = [first, second]
    turn = 0
    while alive:
        for stream in list(alive):
            if stream is second and turn < lead and first in alive:
                continue
            try:
                next(stream)
            except StopIteration:
                alive.remove(stream)
        turn += 1


def chain(
    len_ref, tok_ref, qf_ref, cot_ref, own_hbm, tot_ref, span_ref, recv_ref, wo_ref, bo_ref, g1_ref, s1_ref,
    wup_hbm, bup_ref, wdn_hbm, bdn_ref, g2_ref, s2_ref,
    out_ref, agrad_ref, num_ref, dgm_ref, normed_ref, mixed_ref, ugrad_hbm, vec_ref, sown_ref, stot_ref, sspan_ref, ssend_ref,
    dkeep_ref, dsend_ref,
    st_ref, totp_ref, expand_ref, gather_ref, acc_ref, act_ref, ugrad_ref, dlhs_ref, tmp_ref, wup_ref, wdn_ref, sem,
    *, half, nseg, heads, hdim, chunk, steps, dp_count, sort
):
    step = pl.program_id(0)
    rows, width = tok_ref.shape
    wide = nseg * hdim
    feat = st_ref.shape[1]
    hidden_units = wup_ref.shape[1]
    starts, ends = bounds(len_ref, nseg)
    here = spanning(ends, half)
    x = lax.axis_index("x")
    fetch = [pltpu.make_async_copy(wup_hbm, wup_ref, sem.at[0]), pltpu.make_async_copy(wdn_hbm, wdn_ref, sem.at[1])]
    fetch_own = pltpu.make_async_copy(own_hbm, st_ref, sem.at[2])

    def store(n, side):
        own = hidden_units // 2
        to = ugrad_hbm.at[pl.ds(pl.multiple_of(n * rows, 128), rows), pl.ds(half_cols(side, own), own)]
        return pltpu.make_async_copy(ugrad_ref.at[:, side * own : (side + 1) * own], to, sem.at[3 + side])

    @pl.when(step == 0)
    def _():
        fetch_own.start()
        fetch[0].start()
        fetch[1].start()
        fetch_own.wait()
        vec_ref[...] = jnp.zeros_like(vec_ref)
        acc_ref[...] = jnp.zeros_like(acc_ref)
        put_states(None, tot_ref, span_ref, recv_ref, st_ref, totp_ref, here, nseg, heads, hdim)
        shift = hdim.bit_length() - 1
        lane = iota((256, width), 0) & 127
        expand_ref[:, :width] = as_bf((lane >> 3) == (iota((256, width), 1) >> shift))
        expand_ref[:, width:] = as_bf(((iota((256, 128), 0) & 127) >> 3) == (iota((256, 128), 1) >> 3))
        for k in range(2):
            gather_ref[k * width : (k + 1) * width, :] = as_bf((iota((width, 128), 0) >> shift) == (iota((width, 128), 1) >> 3))
        fetch[0].wait()
        fetch[1].wait()

    def part(lo, size):
        mine = slice(lo, lo + size)
        at = pl.multiple_of(step * rows + lo, 128)
        first = x * half + step * rows + lo
        seg_wide, seg8 = seg_masks(first, size, hdim, nseg, starts, ends)
        low_half = iota((size, 128), 1) < hdim
        nums = []
        for p in range(heads // 2):
            folded = []
            for j in range(2):
                h = 2 * p + j
                r = mm_nt(qf_ref[mine, feat * h : feat * (h + 1)], st_ref[wide * h : wide * (h + 1), :])
                r = jnp.where(seg_wide, r, 0.0)
                folded.append(r[:, :128] + r[:, 128:])
            nums.append(fold_pair(folded, low_half, hdim))
            yield
        numer = jnp.concatenate(nums, axis=1)
        den_parts = split_hi_lo(jnp.where(seg8, mm_nt(qf_ref[mine, :], totp_ref[...]), 0.0))
        yield
        dead = jnp.where(first + iota((size, 128), 0) < ends[-1], 0.0, 1.0)
        spare = jnp.where(iota((size, 128), 1) < 8 * heads, dead, 1.0)
        den_w = mm(den_parts, expand_ref[...])
        inv_c = 1.0 / (den_w[:, width:] + spare)
        inv_w = 1.0 / (den_w[:, :width] + jnp.concatenate([dead] * (width // 128), axis=1))
        yield
        ratio = numer * inv_w
        mixed = ratio.astype(bf16)
        mixed_ref[mine, :] = mixed
        hidden = tok_ref[mine, :].astype(f32) + mm_nt(mixed, wo_ref[...]) + flat_row(bo_ref)
        yield
        scaled1, inverse1 = norm_parts(hidden)
        normed = scaled1 * flat_row(g1_ref) + flat_row(s1_ref)
        normed_bf = normed.astype(bf16)
        normed_ref[mine, :] = normed_bf
        yield

        count = hidden_units // chunk
        cols = [slice(c * chunk, (c + 1) * chunk) for c in range(count)]
        bup = flat_row(bup_ref)
        up = mm(normed_bf, wup_ref[:, cols[0]]) + bup[:, cols[0]]
        branch = normed + flat_row(bdn_ref)
        last = None
        for c in range(count):
            later = mm(normed_bf, wup_ref[:, cols[c + 1]]) + bup[:, cols[c + 1]] if c + 1 < count else None
            act, slope = gelu_parts(up)
            act = act.astype(bf16)
            act_ref[pl.ds(at, size), cols[c]] = act
            ugrad_ref[mine, cols[c]] = slope.astype(bf16)
            if last is not None:
                branch += mm_nt(last, wdn_ref[:, cols[c - 1]])
            last, up = act, later
            yield
        final = branch + mm_nt(last, wdn_ref[:, cols[count - 1]])
        yield
        scaled2, inverse2 = norm_parts(final)
        gain2 = flat_row(g2_ref)
        out_ref[mine, :] = (scaled2 * gain2 + flat_row(s2_ref)).astype(bf16)
        incoming = cot_ref[mine, :].astype(f32)
        grad_final = norm_backward(incoming, scaled2, inverse2, gain2)
        bgrad = grad_final.astype(bf16)
        add_row(vec_ref, 0, grad_final)
        add_row(vec_ref, 1, incoming * scaled2)
        add_row(vec_ref, 2, incoming)
        yield
        put_transposed(dlhs_ref, tmp_ref, bgrad, at, row_sources(dp_count) if sort else [])
        grad_normed = grad_final
        wide_grad = mm(bgrad, wdn_ref[:, cols[0]])
        last = None
        for c in range(count):
            later = mm(bgrad, wdn_ref[:, cols[c + 1]]) if c + 1 < count else None
            ugrad = (wide_grad * ugrad_ref[mine, cols[c]].astype(f32)).astype(bf16)
            ugrad_ref[mine, cols[c]] = ugrad
            sums = jnp.sum(ugrad.astype(f32), axis=0, keepdims=True)
            for k in range(0, chunk, 128):
                row, col = divmod(c * chunk + k, width)
                vec_ref[6 + row : 7 + row, col : col + 128] += sums[:, k : k + 128]
            if last is not None:
                grad_normed += mm_nt(last, wup_ref[:, cols[c - 1]])
            last, wide_grad = ugrad, later
            yield
        grad_normed += mm_nt(last, wup_ref[:, cols[count - 1]])
        yield

        grad_hidden = norm_backward(grad_normed, scaled1, inverse1, flat_row(g1_ref))
        add_row(vec_ref, 3, grad_hidden)
        add_row(vec_ref, 4, grad_normed * scaled1)
        add_row(vec_ref, 5, grad_normed)
        agrad = grad_hidden.astype(bf16)
        agrad_ref[mine, :] = agrad
        yield

        grad_mixed = mm(agrad, wo_ref[...])
        num_grad = (grad_mixed * inv_w).astype(bf16)
        num_ref[mine, :] = num_grad
        inner = split_hi_lo(grad_mixed * ratio)
        yield
        den_m = jnp.where(seg8, -(mm(inner, gather_ref[...]) * inv_c), 0.0).astype(bf16)
        dgm_ref[mine, :] = den_m
        den_t = den_m.T
        masks, _ = lane_segment_masks(first, size, hdim, starts, ends)
        pad = jnp.zeros((8, size), bf16)
        yield
        for p in range(heads // 2):
            num_t = num_grad[:, 128 * p : 128 * (p + 1)].T
            tails = den_t[16 * p : 16 * p + 16, :]
            for j in range(2):
                h = 2 * p + j
                tail = jnp.concatenate([tails[8 * j : 8 * j + 8, :], pad], axis=0)
                lhs = masked_rows(num_t[j * hdim : (j + 1) * hdim, :], masks, tail)
                acc_ref[h] += mm(lhs, qf_ref[mine, feat * h : feat * (h + 1)])
            yield

    @pl.when(jnp.logical_and(step >= 1, step <= steps))
    def _():
        store(step - 1, 0).wait()
        store(step - 1, 1).wait()

    @pl.when(step < steps)
    def _():
        size = rows // 2
        interleave(part(0, size), part(size, size), stream_lead)
        store(step, 0).start()
        store(step, 1).start()

    @pl.when(step == steps - 1)
    def _():
        emit_states(acc_ref, sown_ref, stot_ref, sspan_ref, ssend_ref, here, nseg, heads, hdim)

    own = hidden_units // 2
    count = hidden_units // chunk
    tile = step - steps

    @pl.when(tile >= 0)
    def _():
        xr = tile // (count // 2)
        at = half_cols(xr, own) + (tile - xr * (count // 2)) * chunk
        rhs = act_ref[:, pl.ds(pl.multiple_of(at, 128), chunk)]
        put_grad(dkeep_ref, dsend_ref, mm(dlhs_ref[...], rhs))


def up_out_grads(
    normed_ref, agrad_hbm, mixed_hbm, ugrad_ref,
    *refs,
    count, dp_count, sort
):
    ukeep_ref, usend_ref, okeep_ref, osend_ref, ulhs_ref, olhs_ref, tmp_ref, agrad_ref, mixed_ref, sem = refs[-10:]
    step = pl.program_id(0)
    fetch = [pltpu.make_async_copy(agrad_hbm, agrad_ref, sem.at[0]), pltpu.make_async_copy(mixed_hbm, mixed_ref, sem.at[1])]
    width = normed_ref.shape[1]

    @pl.when(step == 0)
    def _():
        fetch[0].start()
        fetch[1].start()
        put_transposed(ulhs_ref, tmp_ref, normed_ref[...], 0, row_sources(dp_count) if sort else [])

    @pl.when(step < count)
    def _():
        put_grad(ukeep_ref, usend_ref, mm(ulhs_ref[...], ugrad_ref[...]))

    @pl.when(step == count)
    def _():
        fetch[0].wait()
        fetch[1].wait()
        put_transposed(olhs_ref, tmp_ref, agrad_ref[...], 0, row_sources(dp_count) if sort else [])

    @pl.when(step >= count)
    def _():
        rhs = mixed_ref[:, pl.ds(half_cols(step - count, width // 2), width // 2)]
        put_grad(okeep_ref, osend_ref, mm(olhs_ref[...], rhs))


def replicate(pair, low_half, hdim):
    wide = pair.astype(f32)
    other = pltpu.roll(wide, hdim, 1)
    return (jnp.where(low_half, wide, other).astype(bf16), jnp.where(low_half, other, wide).astype(bf16))


def map_back(map_ref, mapg_ref, heads, hdim):
    one, zero = jnp.ones((hdim, map_ref.shape[2]), bf16), jnp.zeros((hdim, map_ref.shape[2]), bf16)
    for p in range(heads // 2):
        left = jnp.concatenate([map_ref[2 * p], zero, one, zero], axis=0)
        right = jnp.concatenate([zero, map_ref[2 * p + 1], zero, one], axis=0)
        mapg_ref[p] = jnp.concatenate([left, right], axis=1)


def rows_grad(logs, mapg, rows_bf, factor):
    r = mm_nt(jnp.concatenate(logs, axis=1), mapg)
    return (factor * r[:, :128] - (factor * factor) * rows_bf.astype(f32) * r[:, 128:]).astype(bf16)


def weight_parts(step, steps, lhs_ref, pg_ref, keep_ref, send_ref, width):
    own = width // 2
    for xr in range(2):

        @pl.when(step == steps + xr)
        def _():
            rhs = [pg_ref[:, pl.ds(c * width + half_cols(xr, own), own)] for c in range(pg_ref.shape[1] // width)]
            put_grad(keep_ref, send_ref, mm(lhs_ref[...], jnp.concatenate(rhs, axis=1)))


def key_back(
    len_ref, kv_ref, tok_ref, map_ref, own_ref, tot_ref, span_ref, recv_ref,
    vec_in, *refs,
    half, nseg, heads, hdim, steps, dp_count, sort, row
):
    pgo_ref, vec_ref, keep_ref, send_ref, sg_ref, sgt_ref, mapg_ref, pg_ref, lhs_ref, tmp_ref = refs[-10:]
    step = pl.program_id(0)
    rows, width = tok_ref.shape
    feat = map_ref.shape[2]
    wide = nseg * hdim
    starts, ends = bounds(len_ref, nseg)
    here = spanning(ends, half)
    first = lax.axis_index("x") * half + step * rows
    factor = hdim ** (-0.25)

    @pl.when(step == 0)
    def _():
        vec_ref[...] = vec_in[...]
        put_states(own_ref, tot_ref, span_ref, recv_ref, sg_ref, sgt_ref, here, nseg, heads, hdim)
        map_back(map_ref, mapg_ref, heads, hdim)

    @pl.when(step < steps)
    def _():
        at = pl.multiple_of(step * rows, 128)
        mine = pl.ds(at, rows)
        seg_wide, seg8 = seg_masks(first, rows, hdim, nseg, starts, ends)
        seg_wide_bf, seg8_bf = as_bf(seg_wide), as_bf(seg8)
        low_half = iota((rows, 128), 1) < hdim
        for p in range(heads // 2):
            k_cols, v_cols = slice(128 * p, 128 * (p + 1)), slice(width + 128 * p, width + 128 * (p + 1))
            k_pair = kv_ref[:, k_cols]
            v_reps = replicate(kv_ref[:, v_cols], low_half, hdim)
            logs, folded = [], []
            for j in range(2):
                h = 2 * p + j
                logits = factor * mm(k_pair, head_map(map_ref, h)) - (0.5 * factor * factor) * key_offset(k_pair, low_half, j)
                feats = jnp.exp(logits)
                lhs = jnp.concatenate([v_reps[j]] * 2, axis=1) * seg_wide_bf
                state_grad = sg_ref[wide * h : wide * (h + 1), :]
                slope = mm(lhs, state_grad) + mm(seg8_bf, sgt_ref[:, feat * h : feat * (h + 1)])
                logs.append((slope * feats).astype(bf16))
                r = jnp.where(seg_wide, mm_nt(feats.astype(bf16), state_grad), 0.0)
                folded.append(r[:, :128] + r[:, 128:])
            pg_ref[mine, k_cols] = rows_grad(logs, mapg_ref[p], k_pair, factor)
            pg_ref[mine, v_cols] = fold_pair(folded, low_half, hdim).astype(bf16)
        grads = pg_ref[mine, :]
        pgo_ref[...] = grads
        add_row(vec_ref, row + 1, grads[:, :width].astype(f32))
        add_row(vec_ref, row + 2, grads[:, width:].astype(f32))
        put_transposed(lhs_ref, tmp_ref, tok_ref[...], at, row_sources(dp_count) if sort else [])

    weight_parts(step, steps, lhs_ref, pg_ref, keep_ref, send_ref, width)


def query_back(
    len_ref, q_ref, num_ref, dgm_ref, tok_ref, map_ref, own_ref, tot_ref, span_ref, recv_ref,
    vec_in, *refs,
    half, nseg, heads, hdim, steps, dp_count, sort, row
):
    pgo_ref, vec_ref, keep_ref, send_ref, st_ref, totp_ref, mapg_ref, pg_ref, lhs_ref, tmp_ref = refs[-10:]
    step = pl.program_id(0)
    rows, width = tok_ref.shape
    feat = map_ref.shape[2]
    wide = nseg * hdim
    starts, ends = bounds(len_ref, nseg)
    first = lax.axis_index("x") * half + step * rows
    factor = hdim ** (-0.25)

    @pl.when(step == 0)
    def _():
        vec_ref[...] = vec_in[...]
        put_states(own_ref, tot_ref, span_ref, recv_ref, st_ref, totp_ref, spanning(ends, half), nseg, heads, hdim)
        map_back(map_ref, mapg_ref, heads, hdim)

    @pl.when(step < steps)
    def _():
        at = pl.multiple_of(step * rows, 128)
        mine = pl.ds(at, rows)
        seg_wide, _ = seg_masks(first, rows, hdim, nseg, starts, ends)
        seg_wide_bf = as_bf(seg_wide)
        low_half = iota((rows, 128), 1) < hdim
        den_m = dgm_ref[...]
        for p in range(heads // 2):
            cols = slice(128 * p, 128 * (p + 1))
            q_pair = q_ref[:, cols]
            reps = replicate(num_ref[:, cols], low_half, hdim)
            logs = []
            for j in range(2):
                h = 2 * p + j
                proj = mm(q_pair, head_map(map_ref, h))
                shifted = proj - jnp.max(proj, axis=-1, keepdims=True)
                lhs = jnp.concatenate([reps[j]] * 2, axis=1) * seg_wide_bf
                slope = mm(lhs, st_ref[wide * h : wide * (h + 1), :]) + mm(den_m, totp_ref[:, feat * h : feat * (h + 1)])
                slope = slope * jnp.exp(factor * shifted)
                peak = jnp.where(shifted == 0.0, 1.0, 0.0)
                share = jnp.sum(slope, axis=-1, keepdims=True) / jnp.sum(peak, axis=-1, keepdims=True)
                logs.append((slope - peak * share).astype(bf16))
            pg_ref[mine, cols] = rows_grad(logs, mapg_ref[p], q_pair, factor)
        grads = pg_ref[mine, :]
        pgo_ref[...] = grads
        add_row(vec_ref, row, grads.astype(f32))
        put_transposed(lhs_ref, tmp_ref, tok_ref[...], at, row_sources(dp_count) if sort else [])

    weight_parts(step, steps, lhs_ref, pg_ref, keep_ref, send_ref, width)


def token_grads(agrad_ref, pgq_ref, pgkv_ref, wq_ref, wk_ref, wv_ref, *refs):
    out_ref = refs[-1]
    width = agrad_ref.shape[1]
    total = agrad_ref[...].astype(f32) + mm_nt(pgq_ref[...], wq_ref[...])
    total += mm_nt(pgkv_ref[:, :width], wk_ref[...])
    out_ref[...] = (total + mm_nt(pgkv_ref[:, width:], wv_ref[...])).astype(bf16)


def params(micros):
    return dict(
        compiler_params=pltpu.CompilerParams(vmem_limit_bytes=vmem_limit),
        cost_estimate=pl.CostEstimate(flops=int(micros * 1.1e9), bytes_accessed=int(micros * 1e6), transcendentals=0),
    )


def whole(shape):
    return pl.BlockSpec(shape, lambda i: (0,) * len(shape), pipeline_mode=pl.Buffered(1))


def resident(shape):
    return pl.BlockSpec(shape, lambda i: (0,) * len(shape))


def sds(shape, dtype):
    return jax.ShapeDtypeStruct(shape, dtype)


every_axis = ("z", "y", "c", "x")


def exchange(values, mask, dp_count):
    return lax.ppermute(values, every_axis, [(i, i ^ mask) for i in range(2 * dp_count)])


def sort_rows(keep, send, dp_count):
    _, _, blocks, quarter, _ = keep.shape
    natural = jnp.stack([keep, send]).transpose(0, 1, 4, 2, 3, 5).reshape(dp_count, -1, 2, blocks, 128)
    rows = jnp.take(natural, jnp.stack(row_sources(dp_count)), axis=0)
    rows = rows.reshape(2, 2, quarter, 2, blocks, 128).transpose(0, 1, 3, 4, 2, 5)
    return rows[0], rows[1]


def route(name, arrays, outs, moves, vec=None, after=()):
    rows = arrays[0].shape[-2]
    grid = 2 if rows % 32 == 0 else 1
    extra, got, send = vec if vec is not None else ([], None, None)
    if vec is not None:
        own = extra[0]
        count, blocks = own.shape[0], own.shape[1] // 128
        assert grid == 2 and 2 * count * blocks == rows

    def spec(shape):
        lead = len(shape) - 2
        return pl.BlockSpec(tuple(shape[:lead]) + (rows // grid, 128), lambda i: (0,) * lead + (i, 0))

    def kernel(*refs):
        ins, results = refs[: len(arrays)], refs[len(arrays) + len(extra) + len(after) :]
        for out, to, parts in moves:
            total = ins[parts[0][0]][parts[0][1]].astype(f32)
            for n, at in parts[1:]:
                total = total + ins[n][at].astype(f32)
            results[out][to] = total.astype(bf16)
        if vec is not None:
            step = pl.program_id(0)
            sums_ref = results[-1]

            @pl.when(step == 0)
            def _():
                sums_ref[...] = functools.reduce(jnp.add, [ref[...] for ref in refs[len(arrays) : len(arrays) + len(extra)]])

            if got is not None:
                other = ins[got[0]][got[1]].astype(f32)
                sums_ref[...] += jnp.concatenate([other[b * count : (b + 1) * count] for b in range(blocks)], axis=1)
            if send is not None:
                sums = sums_ref[...]
                hi = sums.astype(bf16)
                part = jnp.where(step == 0, hi.astype(f32), sums - hi.astype(f32)).astype(bf16)
                rows_of = [part[:, 128 * b : 128 * (b + 1)] for b in range(blocks)]
                results[send[0]][send[1]] = jnp.concatenate(rows_of, axis=0)

    shapes = [sds(v, bf16) for v in outs]
    specs = [spec(v) for v in outs]
    if vec is not None:
        shapes.append(sds(own.shape, f32))
        specs.append(resident(own.shape))
    return pl.pallas_call(
        kernel,
        name=name,
        grid=(grid,),
        in_specs=[spec(a.shape) for a in arrays] + [resident(v.shape) for v in extra] + [pl.BlockSpec(memory_space=pl.ANY)] * len(after),
        out_specs=specs,
        out_shape=shapes,
        **params(3),
    )(*arrays, *extra, *after)


def first_moves(groups, left):
    moves, n = [], 0
    for array, blocks in groups:
        for b in range(blocks):
            for y in range(2):
                for x in range(2):
                    parts = [(array, (y, x, b)), (array + 1, (y, x, b))]
                    moves.append((x, (y, n), parts) if n < left else (2 + y, (x, n - left), parts))
            n += 1
    return moves


def second_moves(array, left, right, out):
    moves = []
    for b in range(left):
        moves += [(out if y == 0 else out + 1, (b,), [(array, (y, b)), (array + 1, (y, b))]) for y in range(2)]
    for b in range(right):
        moves += [(out if x == 0 else out + 2, (left + b if x == 0 else b,), [(array + 2, (x, b)), (array + 3, (x, b))]) for x in range(2)]
    return moves


def third_sum(keep, left_got, right_got):
    return added(bf16, keep, jnp.concatenate([left_got, right_got], axis=0))


def added(dtype, *parts):
    return functools.reduce(jnp.add, [p.astype(f32) for p in parts]).astype(dtype)


def odd_even(part, count):
    pairs = part.reshape(part.shape[0], count // 2, 2, -1, 128)
    return [pairs[:, :, k].reshape(part.shape[0], -1, 128) for k in range(2)]


def columns(part):
    return part.transpose(1, 0, 2).reshape(part.shape[1], -1)


def body(
    tokens, lengths, feature_map, qkv_weight, qkv_bias, out_weight, out_bias, ln1_gain, ln1_shift,
    up_weight, up_bias, down_weight, down_bias, ln2_gain, ln2_shift, cotangent,
):
    half, width = tokens.shape
    heads, hdim, feat = feature_map.shape
    nseg = lengths.shape[1]
    hidden_units = up_weight.shape[1]
    wide = nseg * hdim
    dp_count = lax.axis_size(("z", "y", "c"))
    assert lax.axis_size("x") == 2 and dp_count & (dp_count - 1) == 0 and dp_count >= 8
    assert 2 * hdim == 128 and wide == 256 and 8 * heads <= 128
    sort = (width // dp_count) % 16 == 0
    layout = dict(dp_count=dp_count, sort=sort)
    by_part = qkv_weight.transpose(1, 0, 2)
    rows = min(256, half)
    steps = half // rows
    big = min(512, half)
    big_steps = half // big
    span_rows = heads * hdim + 16
    state_shapes = [
        sds((heads * wide, feat), bf16), sds((heads * 8, feat), f32),
        sds((span_rows - 16, feat), f32), sds((span_rows, feat), bf16),
    ]
    state_specs = [resident(s.shape) for s in state_shapes]
    lens = pl.BlockSpec(memory_space=pltpu.SMEM)
    acc = pltpu.VMEM((heads, wide + 16, feat), f32)
    features = whole(feature_map.shape)
    square = whole((width, width))
    w_specs = [pl.BlockSpec((None, width, width), lambda i, c=c: (c, 0, 0), pipeline_mode=pl.Buffered(1)) for c in range(3)]

    def tile(cols):
        return pl.BlockSpec((rows, cols), lambda i: (jnp.minimum(i, steps - 1), 0))

    def vector(size):
        return pl.BlockSpec((size,), lambda i: (0,))

    static = dict(half=half, nseg=nseg, heads=heads, hdim=hdim)
    dense = 2 * half * width

    def parts(cols, before, count):
        shape = sds((2, 2, cols // 128, width // 4, 128), bf16)
        at = lambda i: (0, jnp.maximum(i - before, 0) // count, 0, 0, 0)
        return [pl.BlockSpec((2, 1, cols // 128, width // 4, 128), at)] * 2, [shape] * 2

    def run(kernel, name, grid, in_specs, args, after, **more):
        fence = [pl.BlockSpec(memory_space=pl.ANY)] * len(after)
        return pl.pallas_call(kernel, name=name, grid=grid, in_specs=list(in_specs) + fence, **more)(*args, *after)

    def over_core(keep, send):
        if not sort:
            keep, send = sort_rows(keep, send, dp_count)
        return keep, exchange(send, 2, dp_count)

    kv, own, tot, span, send = pl.pallas_call(
        functools.partial(forward_keys, **static),
        name="key_states",
        grid=(steps,),
        in_specs=[lens, tile(width), w_specs[1], w_specs[2], whole((3, width)), features],
        out_specs=[tile(2 * width)] + state_specs,
        out_shape=[sds((half, 2 * width), bf16)] + state_shapes,
        scratch_shapes=[acc],
        **params(12),
    )(lengths, tokens, by_part, by_part, qkv_bias, feature_map)
    recv = exchange(send, 1, dp_count)
    q_rows, q_feats = pl.pallas_call(
        functools.partial(forward_queries, heads=heads, hdim=hdim),
        name="query_features",
        grid=(steps,),
        in_specs=[tile(width), w_specs[0], whole((3, width)), features],
        out_specs=[tile(width), tile(heads * feat)],
        out_shape=[sds((half, width), bf16), sds((half, heads * feat), bf16)],
        **params(7),
    )(tokens, by_part, qkv_bias, feature_map)

    chunk = 512
    count = hidden_units // chunk
    half_w, half_u = width // 2, hidden_units // 2
    sum_at = 6 + hidden_units // width
    vec_rows = 16
    assert sum_at + 3 <= vec_rows and 2 * vec_rows * width // 128 == width // 4

    def tiles(cols, size, before):
        per = cols // size

        def at(i):
            t = jnp.clip(i - before, 0, 2 * per - 1)
            return (0, t // per, t % per, 0, 0)

        shape = sds((2, 2, cols // 128, width // 4, 128), bf16)
        return [pl.BlockSpec((2, 1, size // 128, width // 4, 128), at)] * 2, [shape] * 2

    d_specs, d_shapes = tiles(half_u, chunk, big_steps)
    hbm = pl.BlockSpec(memory_space=pl.ANY)

    def big_tile(cols):
        return pl.BlockSpec((big, cols), lambda i: (jnp.minimum(i, big_steps - 1), 0))

    tile_cols = (width, width, width, 128, width, width)
    (output, agrad, num_grad, den_m, normed, mixed, ugrad, vec, s_own, s_tot, s_span, s_send, d_keep, d_send) = run(
        functools.partial(chain, chunk=chunk, steps=big_steps, **layout, **static),
        "chain",
        (big_steps + count,),
        [lens, big_tile(width), big_tile(heads * feat), big_tile(width)]
        + [hbm] + [whole(v.shape) for v in (tot, span, recv)]
        + [square, vector(width), vector(width), vector(width)]
        + [hbm, vector(hidden_units), hbm]
        + [vector(width)] * 3,
        (
            lengths, tokens, q_feats, cotangent, own, tot, span, recv, out_weight, out_bias, ln1_gain, ln1_shift,
            up_weight, up_bias, down_weight, down_bias, ln2_gain, ln2_shift,
        ),
        (),
        out_specs=[big_tile(c) for c in tile_cols] + [hbm, whole((vec_rows, width))] + [whole(v.shape) for v in state_shapes] + d_specs,
        out_shape=[sds((half, c), bf16) for c in tile_cols + (hidden_units,)] + [sds((vec_rows, width), f32)] + state_shapes + d_shapes,
        scratch_shapes=[
            pltpu.VMEM((heads * wide, feat), bf16),
            pltpu.VMEM((128, heads * feat), bf16),
            pltpu.VMEM((256, width + 128), bf16),
            pltpu.VMEM((2 * width, 128), bf16),
            acc,
            pltpu.VMEM((half, hidden_units), bf16),
            pltpu.VMEM((big, hidden_units), bf16),
            pltpu.VMEM((width, half), bf16),
            pltpu.VMEM((width, big // 2), bf16),
            pltpu.VMEM(up_weight.shape, bf16),
            pltpu.VMEM(down_weight.shape, bf16),
            pltpu.SemaphoreType.DMA((5,)),
        ],
        **params(58),
    )
    s_recv = exchange(s_send, 1, dp_count)
    d_keep, d_got = over_core(d_keep, d_send)
    wide_chunk = half_u // 2
    up_count = hidden_units // wide_chunk
    u_specs, u_shapes = tiles(half_u, wide_chunk, 0)
    o_specs, o_shapes = tiles(half_w, half_w, up_count)
    whole_rows = whole((half, width))
    u_keep, u_send, o_keep, o_send = run(
        functools.partial(up_out_grads, count=up_count, **layout),
        "up_out_grads",
        (up_count + 2,),
        [whole_rows, hbm, hbm] + [pl.BlockSpec((half, wide_chunk), lambda i: (0, jnp.minimum(i, up_count - 1)))],
        (normed, agrad, mixed, ugrad),
        (),
        out_specs=u_specs + o_specs,
        out_shape=u_shapes + o_shapes,
        scratch_shapes=[pltpu.VMEM((width, half), bf16)] * 3 + [pltpu.VMEM((half, width), bf16)] * 2 + [pltpu.SemaphoreType.DMA((2,))],
        **params(9),
    )
    u_keep, u_got = over_core(u_keep, u_send)
    o_keep, o_got = over_core(o_keep, o_send)
    block = (width // 4, 128)
    d_n, u_n, o_n = half_u // 128, half_u // 128, half_w // 128
    d_l, uo_l, qkv_n, qkv_l = d_n // 2, (u_n + o_n) // 2, 3 * o_n, 3 * o_n // 2
    d_r, uo_r, qkv_r = d_n - d_l, u_n + o_n - uo_l, qkv_n - qkv_l
    pair = lambda n: (2, n) + block
    d_lk, d_ls, d_rk, d_rs = route("down_1", [d_keep, d_got], [pair(d_l)] * 2 + [pair(d_r)] * 2, first_moves([(0, d_n)], d_l), None, (u_keep, s_recv))
    x_got, y_got = exchange(d_ls, 1, dp_count), exchange(d_rs, 4, dp_count)
    rows = min(512, half)
    steps = half // rows

    def back_scratch(n):
        return [
            pltpu.VMEM((heads // 2, 4 * hdim, 2 * feat), bf16),
            pltpu.VMEM((half, n * width), bf16),
            pltpu.VMEM((width, half), bf16),
            pltpu.VMEM((width, rows), bf16),
        ]

    q_specs, q_shapes = parts(half_w, steps, 1)
    state_scratch = [pltpu.VMEM((heads * wide, feat), bf16), pltpu.VMEM((128, heads * feat), bf16)]
    sums = resident((vec_rows, width))
    sums_shape = sds((vec_rows, width), f32)
    pg_q, vec, q_keep, q_send = run(
        functools.partial(query_back, steps=steps, row=sum_at, **layout, **static),
        "query_back",
        (steps + 2,),
        [lens, tile(width), tile(width), tile(128), tile(width), features] + [whole(v.shape) for v in (own, tot, span, recv)] + [sums],
        (lengths, q_rows, num_grad, den_m, tokens, feature_map, own, tot, span, recv, vec),
        (d_lk,),
        out_specs=[tile(width), sums] + q_specs,
        out_shape=[sds((half, width), bf16), sums_shape] + q_shapes,
        scratch_shapes=state_scratch + back_scratch(1),
        **params(18),
    )
    q_keep, q_got = over_core(q_keep, q_send)
    arrays = [d_lk, x_got, d_rk, y_got, u_keep, u_got, o_keep, o_got]
    moves = second_moves(0, d_l, d_r, 0)
    shift = {1: 4, 2: 3}
    moves = [(shift.get(out, out), at, terms) for out, at, terms in moves]
    for out, at, terms in first_moves([(4, u_n), (6, o_n)], uo_l):
        place = at[0] * (uo_l if out < 2 else uo_r) + at[1]
        if out in (0, 2):
            moves.append((1 if out == 0 else 2, at, terms))
        else:
            moves.append((3, (d_r + place,), terms) if out == 1 else (4, (d_l + place,), terms))
    flat = lambda n: (n,) + block
    d_part, uo_lk, uo_rk, x_send, y_send = route(
        "down_2_up_1", arrays, [flat(d_n), pair(uo_l), pair(uo_r), flat(d_r + 2 * uo_l), flat(d_l + 2 * uo_r)], moves
    )
    x_got, y_got = exchange(x_send, 1, dp_count), exchange(y_send, 4, dp_count)

    kv_specs, kv_shapes = parts(2 * half_w, steps, 1)
    pg_kv, vec, kv_keep, kv_send = run(
        functools.partial(key_back, steps=steps, row=sum_at, **layout, **static),
        "key_back",
        (steps + 2,),
        [lens, tile(2 * width), tile(width), features] + [whole(v.shape) for v in (s_own, s_tot, s_span, s_recv)] + [sums],
        (lengths, kv, tokens, feature_map, s_own, s_tot, s_span, s_recv, vec),
        (d_part,),
        out_specs=[tile(2 * width), sums] + kv_specs,
        out_shape=[sds((half, 2 * width), bf16), sums_shape] + kv_shapes,
        scratch_shapes=state_scratch + back_scratch(2),
        **params(18),
    )
    kv_keep, kv_got = over_core(kv_keep, kv_send)
    vec_got = exchange(vec, 2, dp_count)
    moves = []
    for out, at, terms in second_moves(3, uo_l, uo_r, 0):
        placed = []
        for n, index in terms:
            if n == 4:
                n, index = 1, (d_r + index[0] * uo_l + index[1],)
            elif n == 6:
                n, index = 2, (d_l + index[0] * uo_r + index[1],)
            elif n == 5:
                n = 4
            placed.append((n, index))
        moves.append((out, at, placed))
    d_x, d_y = x_got[:d_r], y_got[:d_l]
    uo_part, uo_ls, uo_rs = route(
        "up_2", [d_part, x_got, y_got, uo_lk, uo_rk], [flat(uo_l + uo_r), flat(uo_l), flat(uo_r)], moves
    )
    x_got, y_got = exchange(uo_rs, 1, dp_count), exchange(uo_ls, 4, dp_count)
    z_bits = [8 << b for b in range((dp_count // 4).bit_length() - 1)]
    left_z = [dp_count // 4 >> n for n in range(len(z_bits))]

    def start_z(part, n):
        keep, send = odd_even(part, left_z[n])
        return keep, exchange(send, z_bits[n], dp_count)

    def end_z(keep, got, n):
        return added(bf16 if n + 1 < len(z_bits) else f32, keep, got)

    down_z = start_z(third_sum(d_part, d_y, d_x), 0)
    qkv_lk, qkv_ls, qkv_rk, qkv_rs, vec = route(
        "qkv_1",
        [q_keep, q_got, kv_keep, kv_got],
        [pair(qkv_l), flat(2 * qkv_l + 1), pair(qkv_r), pair(qkv_r)],
        [
            (out, (at[0] * qkv_l + at[1],) if out == 1 else at, terms)
            for out, at, terms in first_moves([(0, o_n), (2, 2 * o_n)], qkv_l)
        ],
        ([vec, vec_got], None, (1, (2 * qkv_l,))),
        (uo_part,),
    )
    qkv_x, qkv_y = exchange(qkv_ls, 1, dp_count), exchange(qkv_rs, 4, dp_count)

    grad_tokens = run(
        token_grads,
        "token_grads",
        (steps,),
        [tile(width), tile(width), tile(2 * width)] + w_specs,
        (agrad, pg_q, pg_kv, by_part, by_part, by_part),
        (qkv_lk, down_z[0]),
        out_specs=tile(width),
        out_shape=sds((half, width), bf16),
        **params(8),
    )
    up_z = start_z(third_sum(uo_part, y_got, x_got), 0)
    down_part = end_z(*down_z, 0)
    if len(z_bits) > 1:
        down_z = start_z(down_part, 1)
    moves = []
    for out, at, terms in second_moves(0, qkv_l, qkv_r, 0):
        terms = [(n, (at_n[0] * qkv_l + at_n[1],) if n == 1 else at_n) for n, at_n in terms]
        moves.append((out, at, terms))
    qkv_part, qkv_ls, qkv_rs, vec = route(
        "qkv_2",
        [qkv_lk, qkv_x, qkv_rk, qkv_y],
        [flat(qkv_n), flat(qkv_l + 1), flat(qkv_r)],
        moves,
        ([vec], (1, (2 * qkv_l,)), (1, (qkv_l,))),
        (up_z[0], down_z[0], grad_tokens),
    )
    qkv_x, qkv_y = exchange(qkv_rs, 1, dp_count), exchange(qkv_ls, 4, dp_count)

    def rest(part, z, first):
        for n in range(first, len(z_bits)):
            part = end_z(*z, n)
            if n + 1 < len(z_bits):
                z = start_z(part, n + 1)
        return columns(part)

    d_down = rest(down_part, down_z, 1) if len(z_bits) > 1 else columns(down_part)
    d_up_out = rest(None, up_z, 0)

    def add_vec(vec, got):
        count, blocks = vec.shape[0], vec.shape[1] // 128
        got = got.reshape(-1, 128).astype(f32)
        got = got[: count * blocks] + got[count * blocks :]
        return vec + jnp.concatenate([got[b * count : (b + 1) * count] for b in range(blocks)], axis=1)

    def vec_rows_of(vec):
        hi = vec.astype(bf16)
        lo = (vec - hi.astype(f32)).astype(bf16)
        return jnp.concatenate([v[:, 128 * b : 128 * (b + 1)] for v in (hi, lo) for b in range(vec.shape[1] // 128)], axis=0)

    vec = add_vec(vec, qkv_y[qkv_l])
    part = third_sum(qkv_part, qkv_y[:qkv_l], qkv_x)
    for n, bit in enumerate(z_bits):
        keep, send = odd_even(part, left_z[n])
        got = exchange(jnp.concatenate([send.reshape(-1, 128), vec_rows_of(vec)], axis=0), bit, dp_count)
        size = send.size // 128
        vec = add_vec(vec, got[size:])
        part = end_z(keep, got[:size].reshape(send.shape), n)
    d_qkv = part.reshape(3, o_n, -1, 128).transpose(2, 0, 1, 3).reshape(-1, 3, half_w)
    return (
        output,
        grad_tokens,
        d_qkv,
        vec[sum_at : sum_at + 3],
        d_up_out[:, half_u:],
        vec[3],
        vec[4],
        vec[5],
        d_up_out[:, :half_u],
        vec[6:sum_at].reshape(-1),
        d_down,
        vec[0],
        vec[1],
        vec[2],
    )


def solution(mesh):
    dp_count = mesh.shape["dp"]
    fine = jax.sharding.Mesh(mesh.devices.reshape(dp_count // 4, 2, 2, 2), every_axis)
    dp = ("z", "y", "c")
    rows = P(every_axis, None)
    in_specs = (rows, P(dp, None)) + (P(),) * 13 + (rows,)
    out_specs = (
        rows, rows, P(dp, None, "x"), P(), P(dp, "x"), P(), P(), P(),
        P(dp, "x"), P(), P(dp, "x"), P(), P(), P(),
    )
    return jax.shard_map(body, mesh=fine, in_specs=in_specs, out_specs=out_specs, check_vma=False)
```
